128 devices in a mesh: region: 16 (over y, z_hi, core), gx: 4 (over x), gy: 2 (over z_lo).
Axes of the slice: x: 4, y: 4, z: 4 (z_hi: 2, z_lo: 2; z = z_hi * 2 + z_lo), core: 2. Of those that a mesh axis runs over, the one named last changes fastest.
Arguments:
- cap_source: float32 [64, 2048, 1024], P('region', 'gx', 'gy'), may hold values from 0.02 to 2
- cap_sink: float32 [64, 2048, 1024], P('region', 'gx', 'gy'), may hold values from 0.02 to 2
- penalty: float32 [64, 2048, 1024], P('region', 'gx', 'gy'), may hold values from 0.2 to 2
- labels: float32 [64, 2048, 1024], P('region', 'gx', 'gy'), may hold values from 0 to 1
- multiplier: float32 [16, 2048, 1024], P('region', 'gx', 'gy'), may hold values from -3 to 3
Outputs:
- labels_out: float32 [64, 2048, 1024], P('region', 'gx', 'gy')
- multiplier_out: float32 [16, 2048, 1024], P('region', 'gx', 'gy')
The draws below stay inside these ranges and needn't reach their ends.
All inputs are finite; a program needn't handle non-finite values.
Results may differ from the reference program's by a relative error of at most 0.00002.
Values sent between devices are 32-bit elements; how exact they have to be, the bound alone decides.
A program may use at most 256 MiB of HBM per device.

```python
import math
import jax
import jax.numpy as jnp
from jax import lax

CZ = 4
ITERS = 3
NZ = 64
NX = 2048
NY = 1024
N_REGION = 16


def attenuation():
    depth = jnp.arange(NZ).astype(jnp.float32)
    return jnp.exp(-math.log(4.0) * depth / NZ)[:, None, None]


def capacity(key):
    values = jax.random.uniform(key, (NZ, NX, NY), jnp.float32, 0.1, 2.0)
    return values * attenuation()


def draw_cap_source(key, part):
    key = jax.random.fold_in(key, 11)
    return capacity(key).astype(jnp.float32)


def draw_cap_sink(key, part):
    key = jax.random.fold_in(key, 23)
    return capacity(key).astype(jnp.float32)


def draw_labels(key, part):
    key = jax.random.fold_in(key, 37)
    depth = jnp.arange(NZ).astype(jnp.float32)
    spread = (0.15 + 0.35 * depth / NZ)[:, None, None]
    values = jax.random.uniform(key, (NZ, NX, NY), jnp.float32, -1.0, 1.0)
    return (0.5 + spread * values).astype(jnp.float32)


def level_of(key, shape, shards, smallest, top_value):
    level, own = 1.0, jax.random.fold_in(key, 6)
    for position, shards_of in shards:
        steps = jnp.exp(jax.random.uniform(jax.random.fold_in(own, position), (shards_of,), jnp.float32, smallest / len(shards), top_value / len(shards)))
        level = level * jnp.repeat(steps, shape[position] // shards_of).reshape([-1 if axis == position else 1 for axis in range(len(shape))])
    return level


def noise(stream_key, shape, scale, most, split=(), held_as=jnp.bfloat16):
    gain = level_of(stream_key, shape, split, -0.22, 0.18) if split else 1.0
    values = jax.random.normal(stream_key, shape, jnp.float32) * scale * gain
    return jnp.minimum(jnp.maximum(values, -most), most).astype(held_as)


def setup_inputs(seed: int = 0) -> dict:
    keys = jax.random.split(jax.random.key(seed), 6)
    cap_source = draw_cap_source(jax.random.fold_in(keys[5], 71), 0)
    cap_sink = draw_cap_sink(jax.random.fold_in(keys[5], 71), 0)
    penalty = jnp.clip(jnp.exp(math.log(2.0) - 2.3025851 * jax.random.uniform(keys[2], (NZ, NX, NY), jnp.float32) ** level_of(keys[2], (NZ, NX, NY), ((0, 16), (1, 4), (2, 2)), -0.2, 0.2)), 0.2, 2.0)
    labels = draw_labels(jax.random.fold_in(keys[5], 71), 0)
    multiplier = noise(keys[4], (N_REGION, NX, NY), 0.5, 3.0, ((0, 16), (1, 4), (2, 2)), jnp.float32)
    return {"cap_source": cap_source, "cap_sink": cap_sink, "penalty": penalty, "labels": labels, "multiplier": multiplier}


CC = 0.3
STEP = 0.16
RHO = 0.5
EPSILON = 1e-06

def forward(field, axis):
    count = field.shape[axis]
    after = jnp.concatenate([lax.slice_in_dim(field, 1, count, axis=axis), jnp.zeros_like(lax.slice_in_dim(field, 0, 1, axis=axis))], axis)
    shape = [1, 1, 1]
    shape[axis] = count
    mask = (lax.broadcasted_iota(jnp.int32, tuple(shape), axis) < count - 1).astype(field.dtype)
    return (after - field) * mask

def backward(field, axis):
    count = field.shape[axis]
    before = jnp.concatenate([jnp.zeros_like(lax.slice_in_dim(field, 0, 1, axis=axis)), lax.slice_in_dim(field, 0, count - 1, axis=axis)], axis)
    return field - before

def diverge(flow_x, flow_y, flow_z):
    return backward(flow_x, 1) + backward(flow_y, 2) + backward(flow_z, 0)

def solve_slab(inputs):
    source, sink_raw, bound, start, own_plane, below_plane = inputs
    layer = lax.broadcasted_iota(jnp.int32, (CZ, 1, 1), 0)
    sink = sink_raw + jnp.where(layer == CZ - 1, own_plane[None], 0.0) - jnp.where(layer == 0, below_plane[None], 0.0)
    source_flow = jnp.minimum(source, sink)
    sink_flow = source_flow
    flow_x = jnp.zeros_like(source)
    flow_y = jnp.zeros_like(source)
    flow_z = jnp.zeros_like(source)
    divergence = jnp.zeros_like(source)
    field = start
    resid = jnp.zeros_like(source)
    for step in range(ITERS):
        target = divergence - source_flow + sink_flow - field / CC
        new_x = flow_x + STEP * forward(target, 1)
        new_y = flow_y + STEP * forward(target, 2)
        new_z = flow_z + STEP * forward(target, 0)
        magnitude = jnp.sqrt(new_x * new_x + new_y * new_y + new_z * new_z)
        factor = bound / jnp.maximum(magnitude, bound)
        flow_x = new_x * factor
        flow_y = new_y * factor
        flow_z = new_z * factor
        divergence = diverge(flow_x, flow_y, flow_z)
        source_flow = jnp.minimum(source, divergence + sink_flow - field / CC + 1.0 / CC)
        sink_flow = jnp.minimum(sink, source_flow - divergence + field / CC)
        resid = CC * (divergence - source_flow + sink_flow)
        field = field - resid
    return (field, jnp.sum(jnp.abs(resid)))

def reference(cap_source, cap_sink, penalty, labels, multiplier):
    slabs = N_REGION
    valid = (jnp.arange(slabs) < slabs - 1).astype(multiplier.dtype)
    lam = multiplier * valid[:, None, None]
    lam_below = jnp.concatenate([jnp.zeros_like(lam[:1]), lam[:-1]], 0)
    shape = (slabs, CZ, NX, NY)
    fields, sums = lax.map(solve_slab, (cap_source.reshape(shape), cap_sink.reshape(shape), penalty.reshape(shape), labels.reshape(shape), lam, lam_below))
    err = jnp.sum(sums) / (NZ * NX * NY)
    top = fields[:, CZ - 1]
    above = jnp.concatenate([fields[1:, 0], jnp.zeros_like(fields[:1, 0])], 0)
    gap = (top - above) * valid[:, None, None]
    msq = jnp.sum(gap * gap) / ((slabs - 1) * NX * NY)
    rate = RHO * err / jnp.sqrt(msq + EPSILON)
    return (fields.reshape(NZ, NX, NY), lam + rate * gap)
```

```python
import functools

import jax
import jax.numpy as jnp
from jax import lax
from jax.experimental import pallas as pl
from jax.experimental.pallas import tpu as pltpu
from jax.sharding import PartitionSpec as P

MESH = pl.DeviceIdType.MESH
ITERS = 3
CC = 0.3
STEP = 0.16
RHO = 0.5
EPSILON = 1e-06

LANES = 128
TOP = 16
HALO = 8
SLOT = 6
SPAN = 32
GROUPS = 11
WIDE = 176
BLOCK = 128
CHUNKS = 4


def lane_of(rows):
    return lax.broadcasted_iota(jnp.int32, (rows, LANES), 1)


def kernel(
    sizes,
    cap_source,
    cap_sink,
    penalty,
    labels,
    multiplier,
    out,
    mult,
    lab,
    src,
    snk,
    pen,
    px,
    py,
    pz,
    jj,
    pt,
    own_lam,
    low_lam,
    above,
    pack,
    other,
    wl,
    wp,
    ws,
    wk,
    ww,
    wt,
    wpx,
    wpz,
    wj,
    wpy,
    packed,
    packed_low,
    part,
    got_a,
    got_b,
    load_sem,
    lam_load_sem,
    halo_send,
    halo_recv,
    lam_send,
    lam_recv,
    win_send,
    win_recv,
    fwd_send,
    fwd_recv,
    up_send,
    up_recv,
    red_send_a,
    red_recv_a,
    red_send_b,
    red_recv_b,
):
    n_region, n_x, n_y = sizes
    depth, width_x, width_y = labels.shape
    tiles = width_y // LANES
    end = TOP + width_x
    first_row = TOP - HALO
    steps = (width_x + 2 * HALO) // WIDE
    r, x, y = lax.axis_index("region"), lax.axis_index("gx"), lax.axis_index("gy")
    up, down = lax.rem(r + 1, n_region), lax.rem(r + n_region - 1, n_region)
    x_next, x_prev = lax.rem(x + 1, n_x), lax.rem(x + n_x - 1, n_x)
    y_other = 1 - y
    group_a = [(dx, dy) for dx in range(n_x) for dy in range(n_y) if dx or dy]
    peers_a = [(r, lax.rem(x + dx, n_x), lax.rem(y + dy, n_y)) for dx, dy in group_a]
    peers_b = [(lax.rem(r + d, n_region), x, y) for d in range(1, n_region)]

    barrier = pltpu.get_barrier_semaphore()
    for peer in peers_a + peers_b:
        pl.semaphore_signal(barrier, inc=1, device_id=peer, device_id_type=MESH)
    pl.semaphore_wait(barrier, len(peers_a) + len(peers_b))

    def remote(a, b, s, t, device):
        return pltpu.make_async_remote_copy(a, b, s, t, device_id=device, device_id_type=MESH)

    edge_tile = (1 - y) * (tiles - 1)
    arrays = ((labels, lab), (penalty, pen), (cap_source, src), (cap_sink, snk))
    loads = []
    own_copy = pltpu.make_async_copy(multiplier.at[0], own_lam.at[TOP:end], lam_load_sem)
    for i in range(tiles):
        t = lax.rem(edge_tile + i, tiles)
        column = pl.ds(pl.multiple_of(t * LANES, LANES), LANES)
        for q, (whole, held) in enumerate(arrays):
            copy = pltpu.make_async_copy(whole.at[:, :, column], held.at[:, t, TOP:end, :], load_sem.at[q, i])
            copy.start()
            loads.append(copy)
        if i == 0:
            own_copy.start()

    rows_of = width_x // CHUNKS
    lam_copies = []
    for c in range(CHUNKS):
        copy = remote(
            multiplier.at[0, c * rows_of : (c + 1) * rows_of],
            low_lam.at[TOP + c * rows_of : TOP + (c + 1) * rows_of],
            lam_send.at[c],
            lam_recv.at[c],
            (up, x, y),
        )
        copy.start()
        lam_copies.append(copy)

    halo_waits = []
    for side, (device, take, put) in enumerate(
        (
            ((r, x_prev, y), slice(0, HALO), slice(end, end + HALO)),
            ((r, x_next, y), slice(width_x - HALO, width_x), slice(TOP - HALO, TOP)),
        )
    ):
        copy = remote(multiplier.at[0, take], own_lam.at[put], halo_send.at[4, side, 0], halo_recv.at[4, side, 0], device)
        copy.start()
        halo_waits.append(copy)
        for q, (whole, held) in enumerate(arrays):
            for t in range(tiles):
                copy = remote(
                    whole.at[:, take, t * LANES : (t + 1) * LANES],
                    held.at[:, t, put, :],
                    halo_send.at[q, side, t],
                    halo_recv.at[q, side, t],
                    device,
                )
                copy.start()
                halo_waits.append(copy)

    for copy in loads[: len(arrays)]:
        copy.wait()
    own_copy.wait()

    def pack_rows(i, carry):
        row = pl.multiple_of(TOP + i * BLOCK, 8)
        lane = lane_of(BLOCK)
        value = None
        for z in range(depth):
            for q, (_, held) in enumerate(arrays):
                at = SPAN * z + SLOT * q
                moved = pltpu.roll(held[z, edge_tile, pl.ds(row, BLOCK), :], (at + 3) % LANES, 1)
                value = moved if value is None else jnp.where(lane >= at, moved, value)
        at = SPAN * (depth - 1) + SLOT * len(arrays)
        column = pl.ds(pl.multiple_of(edge_tile * LANES, LANES), LANES)
        moved = pltpu.roll(own_lam[pl.ds(row, BLOCK), column], (at + 3) % LANES, 1)
        value = jnp.where(lane >= at, moved, value)
        pack[pl.ds(row, BLOCK), :] = value
        return carry

    lax.fori_loop(0, width_x // BLOCK, pack_rows, 0)
    window = []
    for n, (take, target, put, device) in enumerate(
        (
            (slice(TOP, end), other, slice(TOP, end), (r, x, y_other)),
            (slice(TOP, TOP + HALO), other, slice(end, end + HALO), (r, x_prev, y_other)),
            (slice(end - HALO, end), other, slice(TOP - HALO, TOP), (r, x_next, y_other)),
            (slice(TOP, TOP + HALO), pack, slice(end, end + HALO), (r, x_prev, y)),
            (slice(end - HALO, end), pack, slice(TOP - HALO, TOP), (r, x_next, y)),
        )
    ):
        copy = remote(pack.at[take], target.at[put], win_send.at[n], win_recv.at[n], device)
        copy.start()
        window.append(copy)

    for copy in loads[len(arrays) :]:
        copy.wait()
    for copy in halo_waits:
        copy.wait()
    forwards = []
    for n, put in enumerate((slice(TOP - HALO, TOP), slice(end, end + HALO))):
        copy = remote(own_lam.at[put], low_lam.at[put], fwd_send.at[n], fwd_recv.at[n], (up, x, y))
        copy.start()
        forwards.append(copy)
    for copy in window:
        copy.wait()

    has_above = (r < n_region - 1).astype(jnp.float32)
    has_below = (r > 0).astype(jnp.float32)
    not_first_x = (x > 0).astype(jnp.float32)
    is_last_x = x == n_x - 1
    not_first_y = (y > 0).astype(jnp.float32)
    is_last_y = y == n_y - 1
    lam_lane = SPAN * (depth - 1)

    def make_window(i, carry):
        row = pl.multiple_of(first_row + i * WIDE, 8)
        rows = pl.ds(row, WIDE)
        lane = lane_of(WIDE)
        rest = lane & (SPAN - 1)
        j = rest - SLOT * ((rest * 43) >> 8)
        mine = (j < 3) == (y == 0)
        both = jnp.where(mine, pack[rows, :], other[rows, :])
        wl[rows, :] = both
        wp[rows, :] = pltpu.roll(both, LANES - SLOT, 1)
        ws[rows, :] = pltpu.roll(both, LANES - 2 * SLOT, 1)
        lam = pltpu.roll(both, LANES - 4 * SLOT, 1)
        lam = jnp.where((lane >= lam_lane) & (lane < lam_lane + SLOT), lam * has_above, 0.0)
        wk[rows, :] = pltpu.roll(both, LANES - 3 * SLOT, 1) + lam
        small = lane_of(8)
        for d in range(WIDE // (8 * GROUPS)):
            value = None
            for g in range(GROUPS):
                n = 8 * (d * GROUPS + g)
                moved = pltpu.roll(both[n : n + 8], (8 * g - (lam_lane + 4 * SLOT)) % LANES, 1)
                value = moved if value is None else jnp.where(small >= 8 * g, moved, value)
            at = pl.multiple_of(i * (WIDE // GROUPS) + 8 * d, 8)
            packed[pl.ds(at, 8), :] = value
        return carry

    lax.fori_loop(0, steps, make_window, 0)
    copy = remote(packed, packed_low, fwd_send.at[2], fwd_recv.at[2], (up, x, y))
    copy.start()
    forwards.append(copy)

    def hold_last(ref, *at):
        here = ref[(*at, pl.ds(end, 8), slice(None))]
        last = ref[(*at, pl.ds(end - 1, 8), slice(None))]
        ref[(*at, pl.ds(end, 8), slice(None))] = jnp.where(is_last_x, last, here)

    for z in range(depth):
        for t in range(tiles):
            hold_last(lab, z, t)
    hold_last(wl)

    scale = STEP / CC

    def ascend(k, z, row, count):
        rows, after = pl.ds(row, count), pl.ds(row + 1, count)
        lane = lane_of(count)
        field = jj if k else lab
        side = wj.at[k - 1] if k else wl
        here = [field[z, t, rows, :] for t in range(tiles)]
        rolled = [pltpu.roll(v, LANES - 1, 1) for v in here]
        rolled.append(pltpu.roll(side[rows, :], LANES - 1 - (SPAN * z + 3), 1))
        for t in range(tiles):
            j = here[t]
            jx = field[z, t, after, :]
            jy = jnp.where(lane == LANES - 1, rolled[t + 1], rolled[t])
            if k:
                qx = px[z, t, rows, :] + (jx - j)
                dy = jy - j
            else:
                qx = (j - jx) * scale
                dy = (j - jy) * scale
            if t == tiles - 1:
                dy = jnp.where((lane == LANES - 1) & is_last_y, 0.0, dy)
            qy = py[z, t, rows, :] + dy if k else dy
            square = qx * qx + qy * qy
            if z < depth - 1:
                jz = field[z + 1, t, rows, :]
                qz = pz[z, t, rows, :] + (jz - j) if k else (j - jz) * scale
                square = square + qz * qz
            factor = jnp.minimum(pen[z, t, rows, :] * lax.rsqrt(square), 1.0)
            px[z, t, rows, :] = qx * factor
            py[z, t, rows, :] = qy * factor
            if z < depth - 1:
                pz[z, t, rows, :] = qz * factor

    def ascend_all(k, z):
        def step(i, carry):
            ascend(k, z, pl.multiple_of(first_row + i * WIDE, 8), WIDE)
            return carry

        lax.fori_loop(0, steps, step, 0)
        for t in range(tiles):
            px[z, t, first_row:TOP, :] = px[z, t, first_row:TOP, :] * not_first_x

    def descend(k, z, row, count, total):
        rows, before = pl.ds(row, count), pl.ds(row - 1, count)
        lane = lane_of(count)
        here = [py[z, t, rows, :] for t in range(tiles)]
        rolled = [pltpu.roll(v, 1, 1) for v in here]
        rolled.insert(0, pltpu.roll(wpy[k, rows, :], LANES - (SPAN * z + 2), 1) * not_first_y)
        for t in range(tiles):
            columns = slice(t * LANES, (t + 1) * LANES)
            dv = px[z, t, rows, :] - px[z, t, before, :] + (here[t] - jnp.where(lane == 0, rolled[t], rolled[t + 1]))
            if z < depth - 1:
                dv = dv + pz[z, t, rows, :]
            if z > 0:
                dv = dv - pz[z - 1, t, rows, :]
            source, sink = src[z, t, rows, :], snk[z, t, rows, :]
            if k:
                w, flow = lab[z, t, rows, :], pt[z, t, rows, :]
            else:
                if z == 0:
                    sink = sink - low_lam[rows, columns] * has_below
                if z == depth - 1:
                    sink = sink + own_lam[rows, columns] * has_above
                if z in (0, depth - 1):
                    snk[z, t, rows, :] = sink
                w, flow = lab[z, t, rows, :] * (1.0 / CC), jnp.minimum(source, sink)
            level = jnp.minimum(source - dv + w, flow + 1.0 / CC)
            after = jnp.maximum(level - sink, 0.0)
            if k < ITERS - 1:
                pt[z, t, rows, :] = jnp.minimum(sink, level)
                lab[z, t, rows, :] = after
                jj[z, t, rows, :] = w * STEP - after * (2.0 * STEP)
            else:
                out[z, pl.ds(row - TOP, count), columns] = after * CC
                total = total + jnp.abs(w - after)
        return total

    def descend_all(k, z):
        def step(i, carry):
            descend(k, z, pl.multiple_of(first_row + i * WIDE, 8), WIDE, None)
            return carry

        lax.fori_loop(0, steps, step, 0)
        for t in range(tiles):
            hold_last(jj, z, t)

    def descend_last(z, total):
        def step(i, carry):
            return descend(ITERS - 1, z, pl.multiple_of(TOP + i * BLOCK, 8), BLOCK, carry)

        return lax.fori_loop(0, width_x // BLOCK, step, total)

    side_rows = slice(first_row, end + HALO)
    side_after = slice(first_row + 1, end + HALO + 1)
    side_before = slice(first_row - 1, end + HALO - 1)
    side_lane = lane_of(end + HALO - first_row)

    def ascend_side(k):
        field = wj.at[k - 1] if k else wl
        j = field[side_rows, :]
        jx = field[side_after, :]
        jy = pltpu.roll(j, LANES - 1, 1)
        jz = pltpu.roll(j, LANES - SPAN, 1)
        if k:
            qx = wpx[side_rows, :] + (jx - j)
            qy = wpy[k - 1, side_rows, :] + (jy - j)
            qz = wpz[side_rows, :] + (jz - j)
        else:
            qx, qy, qz = (j - jx) * scale, (j - jy) * scale, (j - jz) * scale
        qz = jnp.where(side_lane < lam_lane, qz, 0.0)
        factor = jnp.minimum(wp[side_rows, :] * lax.rsqrt(qx * qx + qy * qy + qz * qz), 1.0)
        wpx[side_rows, :] = qx * factor
        wpy[k, side_rows, :] = qy * factor
        wpz[side_rows, :] = qz * factor
        wpx[first_row:TOP, :] = wpx[first_row:TOP, :] * not_first_x

    def descend_side(k):
        qy, qz = wpy[k, side_rows, :], wpz[side_rows, :]
        dv = wpx[side_rows, :] - wpx[side_before, :] + (qy - pltpu.roll(qy, 1, 1)) + (qz - pltpu.roll(qz, SPAN, 1))
        source, sink = ws[side_rows, :], wk[side_rows, :]
        if k:
            w, flow = ww[side_rows, :], wt[side_rows, :]
        else:
            w, flow = wl[side_rows, :] * (1.0 / CC), jnp.minimum(source, sink)
        level = jnp.minimum(source - dv + w, flow + 1.0 / CC)
        after = jnp.maximum(level - sink, 0.0)
        wt[side_rows, :] = jnp.minimum(sink, level)
        ww[side_rows, :] = after
        wj[k, side_rows, :] = w * STEP - after * (2.0 * STEP)
        hold_last(wj, k)

    for z in range(depth):
        ascend_all(0, z)
    ascend_side(0)
    for z in range(1, depth):
        descend_all(0, z)

    for copy in forwards:
        copy.wait()
    small = lane_of(8)
    for n in range((width_x + 2 * HALO) // 8):
        d, g = n // GROUPS, n % GROUPS
        lam = pltpu.roll(packed_low[8 * d : 8 * d + 8, :], (LANES - 8 * g) % LANES, 1)
        rows = slice(first_row + 8 * n, first_row + 8 * n + 8)
        wk[rows, :] = wk[rows, :] - jnp.where(small < SLOT, lam * has_below, 0.0)
    descend_side(0)
    ascend_side(1)
    descend_side(1)
    ascend_side(2)

    ascend_all(1, 1)
    for copy in lam_copies:
        copy.wait()
    total = jnp.zeros((BLOCK, LANES), jnp.float32)
    descend_all(0, 0)
    ascend_all(1, 0)
    descend_all(1, 0)
    descend_all_late = functools.partial(descend_all, 1)
    descend_all_late(1)
    ascend_all(2, 0)
    total = descend_last(0, total)
    copy_up = remote(out.at[0], above, up_send, up_recv, (down, x, y))
    copy_up.start()
    ascend_all(1, 2)
    ascend_all(1, 3)
    descend_all(1, 2)
    descend_all(1, 3)
    for z in range(1, depth):
        ascend_all(2, z)
    for z in range(1, depth):
        total = descend_last(z, total)
    copy_up.wait()

    def gap_of(i, carry):
        rows = pl.ds(pl.multiple_of(i * BLOCK, 8), BLOCK)
        gap = (out[depth - 1, rows, :] - above[rows, :]) * has_above
        above[rows, :] = gap
        squares = gap * gap
        for t in range(tiles):
            carry = carry + squares[:, t * LANES : (t + 1) * LANES]
        return carry

    gaps = lax.fori_loop(0, width_x // BLOCK, gap_of, jnp.zeros((BLOCK, LANES), jnp.float32))
    gap_row = jnp.sum(gaps, axis=0, keepdims=True)
    err_row = jnp.sum(total, axis=0, keepdims=True)
    sub = lax.broadcasted_iota(jnp.int32, (8, LANES), 0)
    mine = jnp.where(sub == 0, gap_row, jnp.where(sub == 1, err_row, 0.0))

    for peers, got, send, recv in ((peers_a, got_a, red_send_a, red_recv_a), (peers_b, got_b, red_send_b, red_recv_b)):
        here = part.at[0 if got is got_a else 1]
        here[...] = mine
        copies = []
        for n, peer in enumerate(peers):
            copy = remote(here, got.at[n], send.at[n], recv.at[n], peer)
            copy.start()
            copies.append(copy)
        for copy in copies:
            copy.wait()
        for n in range(len(peers)):
            mine = mine + got[n]

    sums = jnp.sum(mine, axis=1, keepdims=True)
    all_cells = depth * width_x * width_y * n_region * n_x * n_y
    plane_cells = (n_region - 1) * width_x * n_x * width_y * n_y
    err = sums[1:2, :] * (CC / all_cells)
    msq = sums[0:1, :] * (1.0 / plane_cells)
    rate = RHO * err * lax.rsqrt(msq + EPSILON)

    def write(i, carry):
        rows = pl.ds(pl.multiple_of(i * BLOCK, 8), BLOCK)
        lam_rows = pl.ds(pl.multiple_of(TOP + i * BLOCK, 8), BLOCK)
        mult[0, rows, :] = own_lam[lam_rows, :] * has_above + above[rows, :] * rate
        return carry

    lax.fori_loop(0, width_x // BLOCK, write, 0)


def on_device(sizes, cap_source, cap_sink, penalty, labels, multiplier):
    depth, width_x, width_y = labels.shape
    tiles = width_y // LANES
    rows = TOP + width_x + TOP
    n_region, n_x, n_y = sizes

    def vmem(*shape):
        return pltpu.VMEM(shape, jnp.float32)

    def dma(*shape):
        return pltpu.SemaphoreType.DMA(shape) if shape else pltpu.SemaphoreType.DMA

    volume = vmem(depth, tiles, rows, LANES)
    plane = vmem(rows, width_y)
    strip = vmem(rows, LANES)
    peers_a, peers_b = n_x * n_y - 1, n_region - 1
    compact = vmem((width_x + 2 * HALO) // GROUPS, LANES)
    return pl.pallas_call(
        functools.partial(kernel, sizes),
        out_shape=[
            jax.ShapeDtypeStruct(labels.shape, jnp.float32),
            jax.ShapeDtypeStruct(multiplier.shape, jnp.float32),
        ],
        in_specs=[pl.BlockSpec(memory_space=pl.ANY)] * 5,
        out_specs=[pl.BlockSpec(memory_space=pltpu.VMEM)] * 2,
        scratch_shapes=[
            volume,
            volume,
            volume,
            volume,
            volume,
            volume,
            vmem(depth - 1, tiles, rows, LANES),
            volume,
            volume,
            plane,
            plane,
            vmem(width_x, width_y),
            strip,
            strip,
            strip,
            strip,
            strip,
            strip,
            strip,
            strip,
            strip,
            strip,
            vmem(2, rows, LANES),
            vmem(3, rows, LANES),
            compact,
            compact,
            vmem(2, 8, LANES),
            vmem(peers_a, 8, LANES),
            vmem(peers_b, 8, LANES),
            dma(4, tiles),
            dma(),
            dma(5, 2, tiles),
            dma(5, 2, tiles),
            dma(CHUNKS),
            dma(CHUNKS),
            dma(5),
            dma(5),
            dma(3),
            dma(3),
            dma(),
            dma(),
            dma(peers_a),
            dma(peers_a),
            dma(peers_b),
            dma(peers_b),
        ],
        compiler_params=pltpu.CompilerParams(collective_id=0, has_side_effects=True, vmem_limit_bytes=60 << 20),
        name="slab_flow",
    )(cap_source, cap_sink, penalty, labels, multiplier)


def solution(mesh):
    placed = P("region", "gx", "gy")
    sizes = tuple(mesh.shape[a] for a in ("region", "gx", "gy"))
    return jax.shard_map(
        functools.partial(on_device, sizes),
        mesh=mesh,
        in_specs=(placed,) * 5,
        out_specs=(placed, placed),
        check_vma=False,
    )
```

```python
import functools

import jax
import jax.numpy as jnp
from jax import lax
from jax.experimental import pallas as pl
from jax.experimental.pallas import tpu as pltpu
from jax.sharding import PartitionSpec as P

MESH = pl.DeviceIdType.MESH
ITERS = 3
CC = 0.3
STEP = 0.16
RHO = 0.5
EPSILON = 1e-06

LANES = 128
TOP = 32
BOTTOM = 24
HALO = 8
SLOT = 6
SPAN = 32
GROUPS = 11
WIDE = 176
BLOCK = 128
CHUNKS = 4
CHUNK = 136
EARLY = 4


def lane_of(rows):
    return lax.broadcasted_iota(jnp.int32, (rows, LANES), 1)


def kernel(
    sizes,
    cap_source,
    cap_sink,
    penalty,
    labels,
    multiplier,
    out,
    mult,
    lab,
    src,
    snk,
    pen,
    px,
    py,
    pz,
    jj,
    pt,
    own_lam,
    low_lam,
    above,
    halo,
    pack,
    sent,
    other,
    wl,
    wp,
    ws,
    wk,
    ww,
    wt,
    wpx,
    wpz,
    wj,
    wpy,
    packed,
    packed_low,
    part,
    got,
    load_sem,
    lam_load_sem,
    halo_send,
    halo_recv,
    lam_send,
    lam_recv,
    win_send,
    win_recv,
    fwd_send,
    fwd_recv,
    up_send,
    up_recv,
    red_send,
    red_recv,
):
    n_region, n_x, n_y = sizes
    depth, width_x, width_y = labels.shape
    tiles = width_y // LANES
    end = TOP + width_x
    first_row = TOP - HALO
    wide_rows = width_x + 2 * HALO
    steps = wide_rows // WIDE
    r, x, y = lax.axis_index("region"), lax.axis_index("gx"), lax.axis_index("gy")
    up, down = lax.rem(r + 1, n_region), lax.rem(r + n_region - 1, n_region)
    x_next, x_prev = lax.rem(x + 1, n_x), lax.rem(x + n_x - 1, n_x)
    y_other = 1 - y
    core, high, high_y = lax.rem(r, 2), lax.rem(r // 2, 2), r // 4
    n_rows = n_region // 4
    stages = (
        [(4 * high_y + 2 * high + (1 - core), x, y)],
        [(r, lax.rem(x + d, n_x), y) for d in range(1, n_x)],
        [(4 * lax.rem(high_y + d, n_rows) + 2 * high + core, x, y) for d in range(1, n_rows)],
        [
            (r, x, y_other),
            (4 * high_y + 2 * (1 - high) + core, x, y),
            (4 * high_y + 2 * (1 - high) + core, x, y_other),
        ],
    )

    barrier = pltpu.get_barrier_semaphore()
    friends = [(up, x, y), (down, x, y), (up, x, y_other), (down, x, y_other)]
    friends += [peer for stage in stages[1:] for peer in stage]
    for peer in friends:
        pl.semaphore_signal(barrier, inc=1, device_id=peer, device_id_type=MESH)

    def remote(a, b, s, t, device):
        return pltpu.make_async_remote_copy(a, b, s, t, device_id=device, device_id_type=MESH)

    edge_tile = (1 - y) * (tiles - 1)
    arrays = ((labels, lab), (penalty, pen), (cap_source, src), (cap_sink, snk))
    loads = []

    def load(i):
        t = lax.rem(edge_tile + i, tiles)
        column = pl.ds(pl.multiple_of(t * LANES, LANES), LANES)
        for q, (whole, held) in enumerate(arrays):
            copy = pltpu.make_async_copy(whole.at[:, :, column], held.at[:, t, TOP:end, :], load_sem.at[q, i])
            copy.start()
            loads.append(copy)

    own_copy = pltpu.make_async_copy(multiplier.at[0], own_lam.at[TOP:end], lam_load_sem)
    own_copy.start()
    load(0)
    pl.semaphore_wait(barrier, len(friends))

    lam_halo, edge_halo, rest_halo = [], [], []
    sides = (
        ((r, x_prev, y), slice(0, HALO), slice(end, end + HALO)),
        ((r, x_next, y), slice(width_x - HALO, width_x), slice(TOP - HALO, TOP)),
    )
    for side, (device, take, put) in enumerate(sides):
        copy = remote(multiplier.at[0, take], own_lam.at[put], halo_send.at[4, side, 0], halo_recv.at[4, side, 0], device)
        copy.start()
        lam_halo.append(copy)
    lam_bounds = [0] + [CHUNK * c - HALO for c in range(1, CHUNKS)] + [width_x]
    lam_copies = [
        remote(multiplier.at[0, a:b], low_lam.at[TOP + a : TOP + b], lam_send.at[c], lam_recv.at[c], (up, x, y))
        for c, (a, b) in enumerate(zip(lam_bounds[:-1], lam_bounds[1:]))
    ]
    for copy in lam_copies[:EARLY]:
        copy.start()
    edge_column = pl.ds(pl.multiple_of(edge_tile * LANES, LANES), LANES)
    rest_column = pl.ds(pl.multiple_of(y * LANES, LANES), (tiles - 1) * LANES)
    for column, which, copies in ((edge_column, 0, edge_halo), (rest_column, 1, rest_halo)):
        for side, (device, take, put) in enumerate(sides):
            for q, (whole, _) in enumerate(arrays):
                copy = remote(
                    whole.at[:, take, column],
                    halo.at[q, side, :, :, column],
                    halo_send.at[q, side, which],
                    halo_recv.at[q, side, which],
                    device,
                )
                copy.start()
                copies.append(copy)
    for i in range(1, tiles):
        load(i)

    def place_halo(t, column):
        for side, (_, _, put) in enumerate(sides):
            for q, (_, held) in enumerate(arrays):
                for z in range(depth):
                    held[z, t, put, :] = halo[q, side, z, :, column]

    own_copy.wait()
    for copy in lam_halo:
        copy.wait()
    forwards = []
    for n, put in enumerate((slice(TOP - HALO, TOP), slice(end, end + HALO))):
        copy = remote(own_lam.at[put], low_lam.at[put], fwd_send.at[n], fwd_recv.at[n], (up, x, y))
        copy.start()
        forwards.append(copy)
    small = lane_of(8)
    for d in range(wide_rows // (8 * GROUPS)):
        value = None
        for g in range(GROUPS):
            row = first_row + 8 * (d * GROUPS + g)
            moved = pltpu.roll(own_lam[row : row + 8, edge_column], (8 * g + 3) % LANES, 1)
            value = moved if value is None else jnp.where(small >= 8 * g, moved, value)
        packed[8 * d : 8 * d + 8, :] = value
    for n, device in enumerate(((up, x, y), (up, x, y_other))):
        copy = remote(packed, packed_low.at[n], fwd_send.at[2 + n], fwd_recv.at[2 + n], device)
        copy.start()
        forwards.append(copy)

    for copy in loads[: len(arrays)]:
        copy.wait()
    for copy in edge_halo:
        copy.wait()
    place_halo(edge_tile, edge_column)

    def pack_rows(i, carry):
        row = pl.multiple_of(first_row + i * WIDE, 8)
        lane = lane_of(WIDE)
        value = None
        for z in range(depth):
            for q, (_, held) in enumerate(arrays):
                at = SPAN * z + SLOT * q
                moved = pltpu.roll(held[z, edge_tile, pl.ds(row, WIDE), :], (at + 3) % LANES, 1)
                value = moved if value is None else jnp.where(lane >= at, moved, value)
        at = SPAN * (depth - 1) + SLOT * len(arrays)
        moved = pltpu.roll(own_lam[pl.ds(row, WIDE), edge_column], (at + 3) % LANES, 1)
        pack[pl.ds(row, WIDE), :] = jnp.where(lane >= at, moved, value)
        return carry

    lax.fori_loop(0, steps, pack_rows, 0)

    def mine_of(rows):
        rest = lane_of(rows) & (SPAN - 1)
        j = rest - SLOT * ((rest * 43) >> 8)
        return (j < 3) == (y == 0)

    half = wide_rows // 2
    turn = jnp.where(y == 0, 3, LANES - 3)
    lower = pltpu.roll(pack[first_row + half : end + HALO, :], turn, 1)
    sent[...] = jnp.where(mine_of(half), pack[first_row : first_row + half, :], lower)
    window = remote(sent, other, win_send, win_recv, (r, x, y_other))
    window.start()
    for copy in lam_copies[EARLY:]:
        copy.start()

    has_above = (r < n_region - 1).astype(jnp.float32)
    has_below = (r > 0).astype(jnp.float32)
    not_first_x = (x > 0).astype(jnp.float32)
    is_last_x = x == n_x - 1
    not_first_y = (y > 0).astype(jnp.float32)
    is_last_y = y == n_y - 1
    lam_lane = SPAN * (depth - 1)

    for copy in loads[len(arrays) :]:
        copy.wait()
    for copy in rest_halo:
        copy.wait()
    for i in range(1, tiles):
        t = lax.rem(edge_tile + i, tiles)
        place_halo(t, pl.ds(pl.multiple_of(t * LANES, LANES), LANES))

    def hold_last(ref, *at):
        here = ref[(*at, pl.ds(end, 8), slice(None))]
        last = ref[(*at, pl.ds(end - 1, 8), slice(None))]
        ref[(*at, pl.ds(end, 8), slice(None))] = jnp.where(is_last_x, last, here)

    for z in range(depth):
        for t in range(tiles):
            hold_last(lab, z, t)

    window.wait()
    mine = mine_of(half)
    for n in range(2):
        rows = slice(first_row + n * half, first_row + (n + 1) * half)
        theirs = other[...]
        if n:
            theirs = pltpu.roll(theirs, turn, 1)
        both = jnp.where(mine, pack[rows, :], theirs)
        lane = lane_of(half)
        wl[rows, :] = both
        wp[rows, :] = pltpu.roll(both, LANES - SLOT, 1)
        ws[rows, :] = pltpu.roll(both, LANES - 2 * SLOT, 1)
        lam = pltpu.roll(both, LANES - 4 * SLOT, 1)
        lam = jnp.where((lane >= lam_lane) & (lane < lam_lane + SLOT), lam * has_above, 0.0)
        wk[rows, :] = pltpu.roll(both, LANES - 3 * SLOT, 1) + lam
    hold_last(wl)

    scale = STEP / CC

    def ascend(k, z, row, count):
        rows, after = pl.ds(row, count), pl.ds(row + 1, count)
        lane = lane_of(count)
        if k is None:
            field, side = lab, wl
        else:
            field, side = jj, wj.at[k]
        here = [field[z, t, rows, :] for t in range(tiles)]
        rolled = [pltpu.roll(v, LANES - 1, 1) for v in here]
        rolled.append(pltpu.roll(side[rows, :], LANES - 1 - 3 - SPAN * z, 1))
        top = isinstance(z, int) and z == depth - 1
        for t in range(tiles):
            j = here[t]
            jx = field[z, t, after, :]
            jy = jnp.where(lane == LANES - 1, rolled[t + 1], rolled[t])
            dx, dy = (jx - j, jy - j) if k is not None else ((j - jx) * scale, (j - jy) * scale)
            if t == tiles - 1:
                dy = jnp.where((lane == LANES - 1) & is_last_y, 0.0, dy)
            qx, qy = (px[z, t, rows, :] + dx, py[z, t, rows, :] + dy) if k is not None else (dx, dy)
            square = qx * qx + qy * qy
            if not top:
                jz = field[z + 1 if isinstance(z, int) else jnp.minimum(z + 1, depth - 1), t, rows, :]
                qz = pz[z, t, rows, :] + (jz - j) if k is not None else (j - jz) * scale
                square = square + qz * qz
            factor = jnp.minimum(pen[z, t, rows, :] * lax.rsqrt(square), 1.0)
            px[z, t, rows, :] = qx * factor
            py[z, t, rows, :] = qy * factor
            pz[z, t, rows, :] = jnp.zeros_like(square) if top else qz * factor

    def open_x(z):
        for t in range(tiles):
            px[z, t, first_row:TOP, :] = px[z, t, first_row:TOP, :] * not_first_x

    def close_x(z):
        for t in range(tiles):
            hold_last(jj, z, t)

    def descend(k, z, row, count, total=None, check=False):
        rows, before = pl.ds(row, count), pl.ds(row - 1, count)
        lane = lane_of(count)
        here = [py[z, t, rows, :] for t in range(tiles)]
        rolled = [pltpu.roll(v, 1, 1) for v in here]
        rolled.insert(0, pltpu.roll(wpy[k, rows, :], LANES - 2 - SPAN * z, 1) * not_first_y)
        bottom = isinstance(z, int) and z == 0
        top = isinstance(z, int) and z == depth - 1
        if check:
            index = row + lax.broadcasted_iota(jnp.int32, (count, LANES), 0)
            inside = (index >= TOP) & (index < end)
        for t in range(tiles):
            columns = slice(t * LANES, (t + 1) * LANES)
            dv = px[z, t, rows, :] - px[z, t, before, :] + (here[t] - jnp.where(lane == 0, rolled[t], rolled[t + 1]))
            if not top:
                dv = dv + pz[z, t, rows, :]
            if not bottom:
                dv = dv - pz[z - 1, t, rows, :]
            source, sink = src[z, t, rows, :], snk[z, t, rows, :]
            if k:
                w, flow = lab[z, t, rows, :], pt[z, t, rows, :]
            else:
                if bottom:
                    sink = sink - low_lam[rows, columns] * has_below
                if top:
                    sink = sink + own_lam[rows, columns] * has_above
                if bottom or top:
                    snk[z, t, rows, :] = sink
                w, flow = lab[z, t, rows, :] * (1.0 / CC), jnp.minimum(source, sink)
            level = jnp.minimum(source - dv + w, flow + 1.0 / CC)
            after = jnp.maximum(level - sink, 0.0)
            if k < ITERS - 1:
                pt[z, t, rows, :] = jnp.minimum(sink, level)
                lab[z, t, rows, :] = after
                jj[z, t, rows, :] = w * STEP - after * (2.0 * STEP)
            else:
                out[z, rows, columns] = after * CC
                change = jnp.abs(w - after)
                total = total + (jnp.where(inside, change, 0.0) if check else change)
        return total

    def planes(low, high, body, finish):
        def plane(z, carry):
            def step(i, inner):
                body(z, pl.multiple_of(first_row + i * WIDE, 8))
                return inner

            lax.fori_loop(0, steps, step, 0)
            finish(z)
            return carry

        if high - low == 1:
            plane(low, 0)
        else:
            lax.fori_loop(low, high, plane, 0)

    def ascend_planes(k, low, high):
        planes(low, high, lambda z, row: ascend(None if k == 0 else k - 1, z, row, WIDE), open_x)

    def descend_planes(k, low, high):
        planes(low, high, lambda z, row: descend(k, z, row, WIDE), close_x)

    def side_step(body):
        def step(i, carry):
            body(pl.multiple_of(first_row + i * WIDE, 8))
            return carry

        lax.fori_loop(0, steps, step, 0)

    side_lane = lane_of(WIDE)

    def ascend_side(k):
        field = wj.at[k - 1] if k else wl

        def body(row):
            rows, after = pl.ds(row, WIDE), pl.ds(row + 1, WIDE)
            j = field[rows, :]
            jx = field[after, :]
            jy = pltpu.roll(j, LANES - 1, 1)
            jz = pltpu.roll(j, LANES - SPAN, 1)
            if k:
                qx = wpx[rows, :] + (jx - j)
                qy = wpy[k - 1, rows, :] + (jy - j)
                qz = wpz[rows, :] + (jz - j)
            else:
                qx, qy, qz = (j - jx) * scale, (j - jy) * scale, (j - jz) * scale
            qz = jnp.where(side_lane < lam_lane, qz, 0.0)
            factor = jnp.minimum(wp[rows, :] * lax.rsqrt(qx * qx + qy * qy + qz * qz), 1.0)
            wpx[rows, :] = qx * factor
            wpy[k, rows, :] = qy * factor
            wpz[rows, :] = qz * factor

        side_step(body)
        wpx[first_row:TOP, :] = wpx[first_row:TOP, :] * not_first_x

    def descend_side(k):
        def body(row):
            rows, before = pl.ds(row, WIDE), pl.ds(row - 1, WIDE)
            qy, qz = wpy[k, rows, :], wpz[rows, :]
            dv = wpx[rows, :] - wpx[before, :] + (qy - pltpu.roll(qy, 1, 1)) + (qz - pltpu.roll(qz, SPAN, 1))
            source, sink = ws[rows, :], wk[rows, :]
            if k:
                w, flow = ww[rows, :], wt[rows, :]
            else:
                w, flow = wl[rows, :] * (1.0 / CC), jnp.minimum(source, sink)
            level = jnp.minimum(source - dv + w, flow + 1.0 / CC)
            after = jnp.maximum(level - sink, 0.0)
            wt[rows, :] = jnp.minimum(sink, level)
            ww[rows, :] = after
            wj[k, rows, :] = w * STEP - after * (2.0 * STEP)

        side_step(body)
        hold_last(wj, k)

    ascend_planes(0, 0, depth - 1)
    ascend_side(0)
    descend_planes(0, 1, depth - 1)
    for copy in forwards:
        copy.wait()
    low_first = jnp.where(y == 0, 0, 1)
    for n in range(wide_rows // 8):
        d, g = n // GROUPS, n % GROUPS
        rows = slice(first_row + 8 * n, first_row + 8 * n + 8)
        merged = jnp.where(
            small < 8 * g + 3, packed_low[low_first, 8 * d : 8 * d + 8, :], packed_low[1 - low_first, 8 * d : 8 * d + 8, :]
        )
        lam = pltpu.roll(merged, (LANES - 8 * g) % LANES, 1)
        wk[rows, :] = wk[rows, :] - jnp.where(small < SLOT, lam * has_below, 0.0)
    descend_side(0)
    ascend_side(1)
    descend_side(1)
    ascend_side(2)
    ascend_planes(1, 1, 2)

    above_bounds = [0] + [CHUNK * c - 3 * HALO for c in range(1, CHUNKS)] + [width_x]
    above_copies = [
        remote(out.at[0, TOP + a : TOP + b], above.at[a:b], up_send.at[c], up_recv.at[c], (down, x, y))
        for c, (a, b) in enumerate(zip(above_bounds[:-1], above_bounds[1:]))
    ]

    def chunk(c, total):
        for n in range(CHUNKS):

            @pl.when(c == n)
            def _():
                lam_copies[n].wait()

        row = pl.multiple_of(first_row + c * CHUNK, 8)
        descend(0, 0, row, CHUNK)
        close_x(0)
        ascend(0, 0, row - 8, CHUNK)
        open_x(0)
        descend(1, 0, row - 8, CHUNK)
        descend(1, 1, row - 8, CHUNK)
        close_x(0)
        close_x(1)
        ascend(1, 0, row - 16, CHUNK)
        open_x(0)
        total = descend(2, 0, row - 16, CHUNK, total, True)
        for n in range(CHUNKS):

            @pl.when(c == n)
            def _():
                above_copies[n].start()

        return total

    total = lax.fori_loop(0, CHUNKS, chunk, jnp.zeros((CHUNK, LANES), jnp.float32))
    err_row = jnp.sum(total, axis=0, keepdims=True)

    ascend_planes(0, depth - 1, depth)
    descend_planes(0, depth - 1, depth)
    ascend_planes(1, 2, depth)
    descend_planes(1, 2, depth)
    ascend_planes(2, 1, depth)

    def last_plane(z, carry):
        def step(i, inner):
            return descend(ITERS - 1, z, pl.multiple_of(TOP + i * BLOCK, 8), BLOCK, inner)

        return lax.fori_loop(0, width_x // BLOCK, step, carry)

    total = lax.fori_loop(1, depth, last_plane, jnp.zeros((BLOCK, LANES), jnp.float32))
    err_row = err_row + jnp.sum(total, axis=0, keepdims=True)
    for copy in above_copies:
        copy.wait()

    def gap_of(i, carry):
        rows = pl.ds(pl.multiple_of(i * BLOCK, 8), BLOCK)
        gap = (out[depth - 1, pl.ds(pl.multiple_of(TOP + i * BLOCK, 8), BLOCK), :] - above[rows, :]) * has_above
        above[rows, :] = gap
        squares = gap * gap
        for t in range(tiles):
            carry = carry + squares[:, t * LANES : (t + 1) * LANES]
        return carry

    gaps = lax.fori_loop(0, width_x // BLOCK, gap_of, jnp.zeros((BLOCK, LANES), jnp.float32))
    gap_row = jnp.sum(gaps, axis=0, keepdims=True)
    sub = lax.broadcasted_iota(jnp.int32, (8, LANES), 0)
    mine = jnp.where(sub == 0, gap_row, jnp.where(sub == 1, err_row, 0.0))
    n = 0
    for s, stage in enumerate(stages):
        part[s] = mine
        copies = []
        for peer in stage:
            copy = remote(part.at[s], got.at[n], red_send.at[n], red_recv.at[n], peer)
            copy.start()
            copies.append((copy, n))
            n += 1
        for copy, slot in copies:
            copy.wait()
        for copy, slot in copies:
            mine = mine + got[slot]

    sums = jnp.sum(mine, axis=1, keepdims=True)
    all_cells = depth * width_x * width_y * n_region * n_x * n_y
    plane_cells = (n_region - 1) * width_x * n_x * width_y * n_y
    err = sums[1:2, :] * (CC / all_cells)
    msq = sums[0:1, :] * (1.0 / plane_cells)
    rate = RHO * err * lax.rsqrt(msq + EPSILON)

    def write(i, carry):
        rows = pl.ds(pl.multiple_of(i * BLOCK, 8), BLOCK)
        lam_rows = pl.ds(pl.multiple_of(TOP + i * BLOCK, 8), BLOCK)
        mult[0, rows, :] = own_lam[lam_rows, :] * has_above + above[rows, :] * rate
        return carry

    lax.fori_loop(0, width_x // BLOCK, write, 0)


def write_out(held, held_mult, out, mult, sem):
    depth, width_x, _ = out.shape
    copies = [pltpu.make_async_copy(held.at[z, TOP : TOP + width_x], out.at[z], sem.at[z]) for z in range(depth)]
    copies.append(pltpu.make_async_copy(held_mult, mult, sem.at[depth]))
    for copy in copies:
        copy.start()
    for copy in copies:
        copy.wait()


def on_device(sizes, cap_source, cap_sink, penalty, labels, multiplier):
    depth, width_x, width_y = labels.shape
    tiles = width_y // LANES
    rows = TOP + width_x + BOTTOM
    n_region, n_x, n_y = sizes

    def vmem(*shape):
        return pltpu.VMEM(shape, jnp.float32)

    def dma(*shape):
        return pltpu.SemaphoreType.DMA(shape) if shape else pltpu.SemaphoreType.DMA

    volume = vmem(depth, tiles, rows, LANES)
    plane = vmem(rows, width_y)
    strip = vmem(rows, LANES)
    half = vmem(width_x // 2 + HALO, LANES)
    peers = 1 + (n_x - 1) + (n_region // 4 - 1) + 3
    compact = (width_x + 2 * HALO) // GROUPS
    held, held_mult = pl.pallas_call(
        functools.partial(kernel, sizes),
        out_shape=[
            pltpu.VMEM((depth, rows, width_y), jnp.float32),
            pltpu.VMEM(multiplier.shape, jnp.float32),
        ],
        in_specs=[pl.BlockSpec(memory_space=pl.ANY)] * 5,
        out_specs=[pl.BlockSpec(memory_space=pltpu.VMEM)] * 2,
        scratch_shapes=[
            volume,
            volume,
            volume,
            volume,
            volume,
            volume,
            volume,
            volume,
            volume,
            plane,
            plane,
            vmem(width_x, width_y),
            vmem(4, 2, depth, HALO, width_y),
            strip,
            half,
            half,
            strip,
            strip,
            strip,
            strip,
            strip,
            strip,
            strip,
            strip,
            vmem(2, rows, LANES),
            vmem(3, rows, LANES),
            vmem(compact, LANES),
            vmem(2, compact, LANES),
            vmem(4, 8, LANES),
            vmem(peers, 8, LANES),
            dma(4, tiles),
            dma(),
            dma(5, 2, 2),
            dma(5, 2, 2),
            dma(CHUNKS),
            dma(CHUNKS),
            dma(),
            dma(),
            dma(4),
            dma(4),
            dma(CHUNKS),
            dma(CHUNKS),
            dma(peers),
            dma(peers),
        ],
        compiler_params=pltpu.CompilerParams(collective_id=0, has_side_effects=True, vmem_limit_bytes=52 << 20),
        name="slab_flow",
    )(cap_source, cap_sink, penalty, labels, multiplier)
    return pl.pallas_call(
        write_out,
        out_shape=[
            jax.ShapeDtypeStruct(labels.shape, jnp.float32),
            jax.ShapeDtypeStruct(multiplier.shape, jnp.float32),
        ],
        in_specs=[pl.BlockSpec(memory_space=pl.ANY)] * 2,
        out_specs=[pl.BlockSpec(memory_space=pl.ANY)] * 2,
        scratch_shapes=[dma(depth + 1)],
        compiler_params=pltpu.CompilerParams(vmem_limit_bytes=4 << 20),
        name="write_out",
    )(held, held_mult)


def solution(mesh):
    placed = P("region", "gx", "gy")
    sizes = tuple(mesh.shape[a] for a in ("region", "gx", "gy"))
    return jax.shard_map(
        functools.partial(on_device, sizes),
        mesh=mesh,
        in_specs=(placed,) * 5,
        out_specs=(placed, placed),
        check_vma=False,
    )
```

```python
import functools

import jax
import jax.numpy as jnp
from jax import lax
from jax.experimental import pallas as pl
from jax.experimental.pallas import tpu as pltpu
from jax.sharding import PartitionSpec as P

MESH = pl.DeviceIdType.MESH
ITERS = 3
CC = 0.3
STEP = 0.16
RHO = 0.5
EPSILON = 1e-06

LANES = 128
TOP = 32
BOTTOM = 24
HALO = 8
TAKE = 4
SPAN = 32
PART = 10
GROUPS = 11
WIDE = 176
BLOCK = 128
CHUNKS = 4
CHUNK = 136


def lane_of(rows):
    return lax.broadcasted_iota(jnp.int32, (rows, LANES), 1)


def kernel(
    sizes,
    cap_source,
    cap_sink,
    penalty,
    labels,
    multiplier,
    out,
    mult,
    lab,
    src,
    snk,
    pen,
    px,
    py,
    pz,
    jj,
    pt,
    own_lam,
    low_lam,
    above,
    halo,
    sent,
    other,
    wl,
    wp,
    ws,
    wk,
    ww,
    wt,
    wpx,
    wpz,
    wj,
    wpy,
    wu,
    packed,
    packed_low,
    packed_u,
    packed_above,
    part,
    got,
    load_sem,
    lam_load_sem,
    halo_send,
    halo_recv,
    lam_send,
    lam_recv,
    win_send,
    win_recv,
    fwd_send,
    fwd_recv,
    up_send,
    up_recv,
    red_send,
    red_recv,
):
    n_region, n_x, n_y = sizes
    depth, width_x, width_y = labels.shape
    tiles = width_y // LANES
    end = TOP + width_x
    first_row = TOP - HALO
    wide_rows = width_x + 2 * HALO
    steps = wide_rows // WIDE
    r, x, y = lax.axis_index("region"), lax.axis_index("gx"), lax.axis_index("gy")
    up, down = lax.rem(r + 1, n_region), lax.rem(r + n_region - 1, n_region)
    x_next, x_prev = lax.rem(x + 1, n_x), lax.rem(x + n_x - 1, n_x)
    y_other = 1 - y
    core, high, high_y = lax.rem(r, 2), lax.rem(r // 2, 2), r // 4
    n_rows = n_region // 4
    stages = (
        [(4 * high_y + 2 * high + (1 - core), x, y)],
        [(r, lax.rem(x + d, n_x), y) for d in range(1, n_x)],
        [(4 * lax.rem(high_y + d, n_rows) + 2 * high + core, x, y) for d in range(1, n_rows)],
        [
            (r, x, y_other),
            (4 * high_y + 2 * (1 - high) + core, x, y),
            (4 * high_y + 2 * (1 - high) + core, x, y_other),
        ],
    )

    barrier = pltpu.get_barrier_semaphore()
    friends = [(up, x, y), (down, x, y), (up, x, y_other), (down, x, y_other)]
    friends += [peer for stage in stages[1:] for peer in stage]
    for peer in friends:
        pl.semaphore_signal(barrier, inc=1, device_id=peer, device_id_type=MESH)

    def remote(a, b, s, t, device):
        return pltpu.make_async_remote_copy(a, b, s, t, device_id=device, device_id_type=MESH)

    arrays = ((labels, lab), (penalty, pen), (cap_source, src), (cap_sink, snk))
    loads = []

    def load(q):
        whole, held = arrays[q]
        for t in range(tiles):
            column = slice(t * LANES, (t + 1) * LANES)
            copy = pltpu.make_async_copy(whole.at[:, :, column], held.at[:, t, TOP:end, :], load_sem.at[q, t])
            copy.start()
            loads.append(copy)

    load(0)
    load(1)
    pl.semaphore_wait(barrier, len(friends))

    lam_bounds = [0] + [CHUNK * c - HALO for c in range(1, CHUNKS)] + [width_x]
    lam_copies = [
        remote(multiplier.at[0, a:b], low_lam.at[TOP + a : TOP + b], lam_send.at[c], lam_recv.at[c], (up, x, y))
        for c, (a, b) in enumerate(zip(lam_bounds[:-1], lam_bounds[1:]))
    ]
    for copy in lam_copies:
        copy.start()

    sides = (
        ((r, x_prev, y), slice(0, TAKE), slice(0, TAKE), slice(end, end + HALO), slice(end, end + TAKE)),
        ((r, x_next, y), slice(width_x - TAKE, width_x), slice(HALO - TAKE, HALO), slice(TOP - HALO, TOP), slice(TOP - TAKE, TOP)),
    )
    halos = []

    def send_halo(q):
        for side, (device, take, put, _, _) in enumerate(sides):
            copy = remote(arrays[q][0].at[:, take, :], halo.at[q, side, :, put, :], halo_send.at[q, side], halo_recv.at[q, side], device)
            copy.start()
            halos.append(copy)

    def place_halo(q):
        for copy in halos[2 * q : 2 * q + 2]:
            copy.wait()
        for side, (_, _, _, put, _) in enumerate(sides):
            for z in range(depth):
                for t in range(tiles):
                    arrays[q][1][z, t, put, :] = halo[q, side, z, :, t * LANES : (t + 1) * LANES]

    def take_in(q):
        for copy in loads[q * tiles : (q + 1) * tiles]:
            copy.wait()
        place_halo(q)

    send_halo(0)
    send_halo(1)
    load(2)
    load(3)
    own_copy = pltpu.make_async_copy(multiplier.at[0], own_lam.at[TOP:end], lam_load_sem)
    own_copy.start()
    send_halo(2)
    send_halo(3)
    lam_halo = []
    for side, (device, take, _, _, put) in enumerate(sides):
        copy = remote(multiplier.at[0, take], own_lam.at[put], halo_send.at[4, side], halo_recv.at[4, side], device)
        copy.start()
        lam_halo.append(copy)

    has_above = (r < n_region - 1).astype(jnp.float32)
    has_below = (r > 0).astype(jnp.float32)
    not_first_x = (x > 0).astype(jnp.float32)
    is_last_x = x == n_x - 1
    lam_lane = SPAN * (depth - 1)
    edge_tile = (1 - y) * (tiles - 1)
    edge_column = pl.ds(pl.multiple_of(edge_tile * LANES, LANES), LANES)
    small = lane_of(8)

    def turned(value, shift):
        return pltpu.roll(value, lax.rem(shift + 4 * LANES, LANES), 1)

    def hold_last(ref, *at):
        here = ref[(*at, pl.ds(end, 8), slice(None))]
        last = ref[(*at, pl.ds(end - 1, 8), slice(None))]
        ref[(*at, pl.ds(end, 8), slice(None))] = jnp.where(is_last_x, last, here)

    scale = STEP / CC

    def ascend(k, z, row, count):
        rows, after = pl.ds(row, count), pl.ds(row + 1, count)
        lane = lane_of(count)
        field = lab if k == 0 else jj
        here = [field[z, t, rows, :] for t in range(tiles)]
        rolled = [pltpu.roll(v, LANES - 1, 1) for v in here]
        for t in range(tiles):
            j = here[t]
            jx = field[z, t, after, :]
            jy = jnp.where(lane == LANES - 1, rolled[t + 1] if t < tiles - 1 else j, rolled[t])
            dx, dy = (jx - j, jy - j) if k else ((j - jx) * scale, (j - jy) * scale)
            qx, qy = (px[z, t, rows, :] + dx, py[z, t, rows, :] + dy) if k else (dx, dy)
            square = qx * qx + qy * qy
            jz = field[jnp.minimum(z + 1, depth - 1), t, rows, :]
            qz = pz[z, t, rows, :] + (jz - j) if k else (j - jz) * scale
            square = square + qz * qz
            factor = jnp.minimum(pen[z, t, rows, :] * lax.rsqrt(square), 1.0)
            px[z, t, rows, :] = qx * factor
            py[z, t, rows, :] = qy * factor
            pz[z, t, rows, :] = qz * factor

    def open_x(z):
        for t in range(tiles):
            px[z, t, first_row:TOP, :] = px[z, t, first_row:TOP, :] * not_first_x

    def close_x(z):
        for t in range(tiles):
            hold_last(jj, z, t)

    def descend(k, z, row, count, total=None, check=False):
        rows, before = pl.ds(row, count), pl.ds(row - 1, count)
        lane = lane_of(count)
        here = [py[z, t, rows, :] for t in range(tiles)]
        rolled = [pltpu.roll(v, 1, 1) for v in here]
        bottom = isinstance(z, int) and z == 0
        top = isinstance(z, int) and z == depth - 1
        if check:
            index = row + lax.broadcasted_iota(jnp.int32, (count, LANES), 0)
            inside = (index >= TOP) & (index < end)
        for t in range(tiles):
            columns = slice(t * LANES, (t + 1) * LANES)
            dv = px[z, t, rows, :] - px[z, t, before, :] + (here[t] - jnp.where(lane == 0, rolled[t - 1] if t else 0.0, rolled[t]))
            if not top:
                dv = dv + pz[z, t, rows, :]
            if not bottom:
                dv = dv - pz[z - 1, t, rows, :]
            source, sink = src[z, t, rows, :], snk[z, t, rows, :]
            if k:
                w, flow = lab[z, t, rows, :], pt[z, t, rows, :]
            else:
                if bottom:
                    sink = sink - low_lam[rows, columns] * has_below
                if top:
                    sink = sink + own_lam[rows, columns] * has_above
                if bottom or top:
                    snk[z, t, rows, :] = sink
                w, flow = lab[z, t, rows, :] * (1.0 / CC), jnp.minimum(source, sink)
            level = jnp.minimum(source - dv + w, flow + 1.0 / CC)
            after = jnp.maximum(level - sink, 0.0)
            if k < ITERS - 1:
                pt[z, t, rows, :] = jnp.minimum(sink, level)
                lab[z, t, rows, :] = after
                jj[z, t, rows, :] = w * STEP - after * (2.0 * STEP)
            else:
                out[z, rows, columns] = after * CC
                change = jnp.abs(w - after)
                if t == 0:
                    change = jnp.where((lane < 3) & (y == 1), 0.0, change)
                if t == tiles - 1:
                    change = jnp.where((lane >= LANES - 3) & (y == 0), 0.0, change)
                total = total + (jnp.where(inside, change, 0.0) if check else change)
        return total

    def planes(low, high, body, finish):
        def plane(z, carry):
            def step(i, inner):
                body(z, pl.multiple_of(first_row + i * WIDE, 8))
                return inner

            lax.fori_loop(0, steps, step, 0)
            finish(z)
            return carry

        if high - low == 1:
            plane(low, 0)
        else:
            lax.fori_loop(low, high, plane, 0)

    def ascend_planes(k, low, high):
        planes(low, high, lambda z, row: ascend(k, z, row, WIDE), open_x)

    def descend_planes(k, low, high):
        planes(low, high, lambda z, row: descend(k, z, row, WIDE), close_x)

    def side_step(body):
        def step(i, carry):
            body(pl.multiple_of(first_row + i * WIDE, 8))
            return carry

        lax.fori_loop(0, steps, step, 0)

    side_lane = lane_of(WIDE)

    def ascend_side(k):
        field = wj.at[k - 1] if k else wl

        def body(row):
            rows, after = pl.ds(row, WIDE), pl.ds(row + 1, WIDE)
            j = field[rows, :]
            jx = field[after, :]
            jy = pltpu.roll(j, LANES - 1, 1)
            jz = pltpu.roll(j, LANES - SPAN, 1)
            if k:
                qx = wpx[rows, :] + (jx - j)
                qy = wpy[k - 1, rows, :] + (jy - j)
                qz = wpz[rows, :] + (jz - j)
            else:
                qx, qy, qz = (j - jx) * scale, (j - jy) * scale, (j - jz) * scale
            qz = jnp.where(side_lane < lam_lane, qz, 0.0)
            factor = jnp.minimum(wp[rows, :] * lax.rsqrt(qx * qx + qy * qy + qz * qz), 1.0)
            wpx[rows, :] = qx * factor
            wpy[k, rows, :] = qy * factor
            wpz[rows, :] = qz * factor

        side_step(body)
        wpx[first_row:TOP, :] = wpx[first_row:TOP, :] * not_first_x

    def descend_side(k, total=None):
        def body(row):
            rows, before = pl.ds(row, WIDE), pl.ds(row - 1, WIDE)
            qy, qz = wpy[k, rows, :], wpz[rows, :]
            dv = wpx[rows, :] - wpx[before, :] + (qy - pltpu.roll(qy, 1, 1)) + (qz - pltpu.roll(qz, SPAN, 1))
            source, sink = ws[rows, :], wk[rows, :]
            if k:
                w, flow = ww[rows, :], wt[rows, :]
            else:
                w, flow = wl[rows, :] * (1.0 / CC), jnp.minimum(source, sink)
            level = jnp.minimum(source - dv + w, flow + 1.0 / CC)
            after = jnp.maximum(level - sink, 0.0)
            if k < ITERS - 1:
                wt[rows, :] = jnp.minimum(sink, level)
                ww[rows, :] = after
                wj[k, rows, :] = w * STEP - after * (2.0 * STEP)
            else:
                wu[rows, :] = after * CC
                j = side_lane & (SPAN - 1)
                index = row + lax.broadcasted_iota(jnp.int32, (WIDE, LANES), 0)
                inside = (j >= 3) & (j < 6) & (index >= TOP) & (index < end)
                ww[rows, :] = jnp.where(inside, jnp.abs(w - after), 0.0)

        side_step(body)
        if k < ITERS - 1:
            hold_last(wj, k)

    take_in(0)
    take_in(1)
    for z in range(depth):
        for t in range(tiles):
            hold_last(lab, z, t)
    ascend_planes(0, 0, depth)
    take_in(2)
    take_in(3)
    own_copy.wait()
    for copy in lam_halo:
        copy.wait()
    forwards = []
    for n, (_, _, _, _, put) in enumerate(sides):
        copy = remote(own_lam.at[put], low_lam.at[put], fwd_send.at[n], fwd_recv.at[n], (up, x, y))
        copy.start()
        forwards.append(copy)

    def own_window(row):
        rows = pl.ds(row, WIDE)
        for (_, held), strip in zip(arrays, (wl, wp, ws, wk)):
            value = None
            for z in range(depth):
                moved = turned(held[z, edge_tile, rows, :], SPAN * z + 6 - 3 * y)
                value = moved if value is None else jnp.where(side_lane >= SPAN * z, moved, value)
            if strip is wk:
                moved = turned(own_lam[rows, edge_column], lam_lane + 6 - 3 * y)
                value = value + jnp.where(side_lane >= lam_lane, moved * has_above, 0.0)
            strip[rows, :] = value

    side_step(own_window)
    for d in range(wide_rows // (8 * GROUPS)):
        value = None
        for g in range(GROUPS):
            row = first_row + 8 * (d * GROUPS + g)
            moved = turned(own_lam[row : row + 8, edge_column], 8 * g + 6 - 6 * y)
            value = moved if value is None else jnp.where(small >= 8 * g, moved, value)
        packed[8 * d : 8 * d + 8, :] = value
    for n, device in enumerate(((up, x, y), (up, x, y_other))):
        copy = remote(packed, packed_low.at[n], fwd_send.at[2 + n], fwd_recv.at[2 + n], device)
        copy.start()
        forwards.append(copy)

    def pack_window(i, carry):
        off = lane_of(WIDE // 2) & (SPAN - 1)
        value = None
        for g in range(steps):
            rows = pl.ds(pl.multiple_of(first_row + WIDE * g + i * (WIDE // 2), 8), WIDE // 2)
            moves = ((wl, 0, -3), (wp, 3, 0), (ws, 6, 2 + y), (wk, 8, 4 + y))
            for strip, at, shift in moves:
                moved = turned(strip[rows, :], PART * g + shift)
                value = moved if value is None else jnp.where(off >= PART * g + at, moved, value)
        sent[pl.ds(pl.multiple_of(i * (WIDE // 2), 8), WIDE // 2), :] = value
        return carry

    lax.fori_loop(0, 2, pack_window, 0)
    window = remote(sent, other, win_send, win_recv, (r, x, y_other))
    window.start()
    descend_planes(0, 1, depth - 1)
    ascend_planes(1, 1, 2)

    above_bounds = [0] + [CHUNK * c - 3 * HALO for c in range(1, CHUNKS)] + [width_x]
    above_copies = [
        remote(out.at[0, TOP + a : TOP + b], above.at[a:b], up_send.at[c], up_recv.at[c], (down, x, y))
        for c, (a, b) in enumerate(zip(above_bounds[:-1], above_bounds[1:]))
    ]

    for copy in forwards:
        copy.wait()

    def chunk(c, total):
        for n in range(CHUNKS):

            @pl.when(c == n)
            def _():
                lam_copies[n].wait()

        row = pl.multiple_of(first_row + c * CHUNK, 8)
        descend(0, 0, row, CHUNK)
        close_x(0)
        ascend(1, 0, row - 8, CHUNK)
        open_x(0)
        descend(1, 0, row - 8, CHUNK)
        descend(1, 1, row - 8, CHUNK)
        close_x(0)
        close_x(1)
        ascend(2, 0, row - 16, CHUNK)
        open_x(0)
        total = descend(2, 0, row - 16, CHUNK, total, True)
        for n in range(CHUNKS):

            @pl.when(c == n)
            def _():
                above_copies[n].start()

        return total

    total = lax.fori_loop(0, CHUNKS, chunk, jnp.zeros((CHUNK, LANES), jnp.float32))
    err_row = jnp.sum(total, axis=0, keepdims=True)

    window.wait()
    for g in range(steps):
        rows = slice(first_row + WIDE * g, first_row + WIDE * (g + 1))
        off = side_lane & (SPAN - 1)
        theirs = (off >= 6 - 6 * y) & (off < 9 - 6 * y)
        moves = ((wl, 6 - 6 * y), (wp, 3 - 6 * y), (ws, -5 * y), (wk, -2 - 5 * y))
        for strip, shift in moves:
            strip[rows, :] = jnp.where(theirs, turned(other[...], shift - PART * g), strip[rows, :])
    hold_last(wl)
    for n in range(wide_rows // 8):
        d, g = n // GROUPS, n % GROUPS
        rows = slice(first_row + 8 * n, first_row + 8 * n + 8)
        same = turned(packed_low[0, 8 * d : 8 * d + 8, :], 3 * y - 8 * g)
        cross = turned(packed_low[1, 8 * d : 8 * d + 8, :], 6 - 9 * y - 8 * g)
        theirs = (small >= 6 - 6 * y) & (small < 9 - 6 * y)
        lam = jnp.where(theirs, cross, same)
        wk[rows, :] = wk[rows, :] - jnp.where(small < 9, lam * has_below, 0.0)
    for k in range(ITERS):
        ascend_side(k)
        descend_side(k)
    for d in range(wide_rows // (8 * GROUPS)):
        value = None
        for g in range(GROUPS):
            row = first_row + 8 * (d * GROUPS + g)
            moved = pltpu.roll(wu[row : row + 8, :], 8 * g, 1)
            value = moved if value is None else jnp.where(small >= 8 * g, moved, value)
        packed_u[8 * d : 8 * d + 8, :] = value
    down_copy = remote(packed_u, packed_above, fwd_send.at[4], fwd_recv.at[4], (down, x, y))
    down_copy.start()
    err_row = err_row + jnp.sum(ww[first_row : end + HALO, :], axis=0, keepdims=True)

    descend_planes(0, depth - 1, depth)
    ascend_planes(1, 2, depth)
    descend_planes(1, 2, depth)
    ascend_planes(2, 1, depth)

    def last_plane(z, carry):
        def step(i, inner):
            return descend(ITERS - 1, z, pl.multiple_of(TOP + i * BLOCK, 8), BLOCK, inner)

        return lax.fori_loop(0, width_x // BLOCK, step, carry)

    total = lax.fori_loop(1, depth, last_plane, jnp.zeros((BLOCK, LANES), jnp.float32))
    err_row = err_row + jnp.sum(total, axis=0, keepdims=True)

    def edge_of(rows):
        lane = lane_of(rows)
        return (lane >= (1 - y) * (LANES - 3)) & (lane < (1 - y) * (LANES - 3) + 3)

    def patch(z):
        moved = turned(wu[TOP:end, :], 122 - 125 * y - SPAN * z)
        out[z, TOP:end, edge_column] = jnp.where(edge_of(width_x), moved, out[z, TOP:end, edge_column])

    for z in range(1, depth):
        patch(z)
    down_copy.wait()

    gaps = jnp.zeros((8, LANES), jnp.float32)
    edge = edge_of(8)
    for copy, a, b in zip(above_copies, above_bounds[:-1], above_bounds[1:]):
        copy.wait()
        for row in range(a, b, 8):
            n = row // 8 + 1
            d, g = n // GROUPS, n % GROUPS
            moved = turned(packed_above[8 * d : 8 * d + 8, :], 122 - 125 * y - 8 * g)
            above[row : row + 8, edge_column] = jnp.where(edge, moved, above[row : row + 8, edge_column])
        gap = (out[depth - 1, TOP + a : TOP + b, :] - above[a:b, :]) * has_above
        above[a:b, :] = gap
        squares = gap * gap
        for row in range(0, b - a, 8):
            for t in range(tiles):
                gaps = gaps + squares[row : row + 8, t * LANES : (t + 1) * LANES]
    gap_row = jnp.sum(gaps, axis=0, keepdims=True)
    sub = lax.broadcasted_iota(jnp.int32, (8, LANES), 0)
    mine = jnp.where(sub == 0, gap_row, jnp.where(sub == 1, err_row, 0.0))
    n = 0
    for s, stage in enumerate(stages):
        part[s] = mine
        copies = []
        for peer in stage:
            copy = remote(part.at[s, 0:2], got.at[n, 0:2], red_send.at[n], red_recv.at[n], peer)
            copy.start()
            copies.append((copy, n))
            n += 1
        if s == len(stages) - 1:
            patch(0)
        for copy, slot in copies:
            copy.wait()
        for copy, slot in copies:
            mine = mine + got[slot]

    sums = jnp.sum(mine, axis=1, keepdims=True)
    all_cells = depth * width_x * width_y * n_region * n_x * n_y
    plane_cells = (n_region - 1) * width_x * n_x * width_y * n_y
    err = sums[1:2, :] * (CC / all_cells)
    msq = sums[0:1, :] * (1.0 / plane_cells)
    rate = RHO * err * lax.rsqrt(msq + EPSILON)

    def write(i, carry):
        rows = pl.ds(pl.multiple_of(i * BLOCK, 8), BLOCK)
        lam_rows = pl.ds(pl.multiple_of(TOP + i * BLOCK, 8), BLOCK)
        mult[0, rows, :] = own_lam[lam_rows, :] * has_above + above[rows, :] * rate
        return carry

    lax.fori_loop(0, width_x // BLOCK, write, 0)


def write_out(held, held_mult, out, mult, sem):
    depth, width_x, _ = out.shape
    copies = [pltpu.make_async_copy(held.at[z, TOP : TOP + width_x], out.at[z], sem.at[z]) for z in range(depth)]
    copies.append(pltpu.make_async_copy(held_mult, mult, sem.at[depth]))
    for copy in copies:
        copy.start()
    for copy in copies:
        copy.wait()


def on_device(sizes, cap_source, cap_sink, penalty, labels, multiplier):
    depth, width_x, width_y = labels.shape
    tiles = width_y // LANES
    rows = TOP + width_x + BOTTOM
    n_region, n_x, n_y = sizes

    def vmem(*shape):
        return pltpu.VMEM(shape, jnp.float32)

    def dma(*shape):
        return pltpu.SemaphoreType.DMA(shape) if shape else pltpu.SemaphoreType.DMA

    volume = vmem(depth, tiles, rows, LANES)
    plane = vmem(rows, width_y)
    strip = vmem(rows, LANES)
    third = vmem((width_x + 2 * HALO) // 3, LANES)
    peers = 1 + (n_x - 1) + (n_region // 4 - 1) + 3
    compact = (width_x + 2 * HALO) // GROUPS
    held, held_mult = pl.pallas_call(
        functools.partial(kernel, sizes),
        out_shape=[
            pltpu.VMEM((depth, rows, width_y), jnp.float32),
            pltpu.VMEM(multiplier.shape, jnp.float32),
        ],
        in_specs=[pl.BlockSpec(memory_space=pl.ANY)] * 5,
        out_specs=[pl.BlockSpec(memory_space=pltpu.VMEM)] * 2,
        scratch_shapes=[
            volume,
            volume,
            volume,
            volume,
            volume,
            volume,
            volume,
            volume,
            volume,
            plane,
            plane,
            vmem(width_x, width_y),
            vmem(4, 2, depth, HALO, width_y),
            third,
            third,
            strip,
            strip,
            strip,
            strip,
            strip,
            strip,
            strip,
            strip,
            vmem(2, rows, LANES),
            vmem(3, rows, LANES),
            strip,
            vmem(compact, LANES),
            vmem(2, compact, LANES),
            vmem(compact, LANES),
            vmem(compact, LANES),
            vmem(4, 8, LANES),
            vmem(peers, 8, LANES),
            dma(4, tiles),
            dma(),
            dma(5, 2),
            dma(5, 2),
            dma(CHUNKS),
            dma(CHUNKS),
            dma(),
            dma(),
            dma(5),
            dma(5),
            dma(CHUNKS),
            dma(CHUNKS),
            dma(peers),
            dma(peers),
        ],
        compiler_params=pltpu.CompilerParams(collective_id=0, has_side_effects=True, vmem_limit_bytes=52 << 20),
        name="slab_flow",
    )(cap_source, cap_sink, penalty, labels, multiplier)
    return pl.pallas_call(
        write_out,
        out_shape=[
            jax.ShapeDtypeStruct(labels.shape, jnp.float32),
            jax.ShapeDtypeStruct(multiplier.shape, jnp.float32),
        ],
        in_specs=[pl.BlockSpec(memory_space=pl.ANY)] * 2,
        out_specs=[pl.BlockSpec(memory_space=pl.ANY)] * 2,
        scratch_shapes=[dma(depth + 1)],
        compiler_params=pltpu.CompilerParams(vmem_limit_bytes=4 << 20),
        name="write_out",
    )(held, held_mult)


def solution(mesh):
    placed = P("region", "gx", "gy")
    sizes = tuple(mesh.shape[a] for a in ("region", "gx", "gy"))
    return jax.shard_map(
        functools.partial(on_device, sizes),
        mesh=mesh,
        in_specs=(placed,) * 5,
        out_specs=(placed, placed),
        check_vma=False,
    )
```

```python
import functools

import jax
import jax.numpy as jnp
from jax import lax
from jax.experimental import pallas as pl
from jax.experimental.pallas import tpu as pltpu
from jax.sharding import PartitionSpec as P

MESH = pl.DeviceIdType.MESH
ITERS = 3
CC = 0.3
STEP = 0.16
RHO = 0.5
EPSILON = 1e-06

LANES = 128
TOP = 32
BOTTOM = 24
HALO = 8
TAKE = 4
SPAN = 32
PART = 10
GROUPS = 11
WIDE = 176
BLOCK = 128
CHUNKS = 4
CHUNK = 136


def lane_of(rows):
    return lax.broadcasted_iota(jnp.int32, (rows, LANES), 1)


def kernel(
    sizes,
    cap_source,
    cap_sink,
    penalty,
    labels,
    multiplier,
    out,
    mult,
    lab,
    src,
    snk,
    pen,
    px,
    py,
    pz,
    jj,
    pt,
    own_lam,
    low_lam,
    above,
    halo,
    sent,
    other,
    wl,
    wp,
    ws,
    wk,
    ww,
    wt,
    wpx,
    wpz,
    wj,
    wpy,
    wu,
    packed,
    packed_low,
    packed_u,
    packed_above,
    part,
    got_near,
    got_far,
    load_sem,
    lam_load_sem,
    halo_send,
    halo_recv,
    lam_send,
    lam_recv,
    win_send,
    win_recv,
    fwd_send,
    fwd_recv,
    up_send,
    up_recv,
    red_send,
    red_recv,
):
    n_region, n_x, n_y = sizes
    depth, width_x, width_y = labels.shape
    tiles = width_y // LANES
    end = TOP + width_x
    first_row = TOP - HALO
    wide_rows = width_x + 2 * HALO
    steps = wide_rows // WIDE
    r, x, y = lax.axis_index("region"), lax.axis_index("gx"), lax.axis_index("gy")
    up, down = lax.rem(r + 1, n_region), lax.rem(r + n_region - 1, n_region)
    x_next, x_prev = lax.rem(x + 1, n_x), lax.rem(x + n_x - 1, n_x)
    y_other = 1 - y
    core, high, high_y = lax.rem(r, 2), lax.rem(r // 2, 2), r // 4
    n_rows = n_region // 4
    near, far = [], []
    for dx in range(n_x):
        for dc in range(2):
            if dx or dc:
                at = (4 * high_y + 2 * high + lax.rem(core + dc, 2), lax.rem(x + dx, n_x), y)
                near.append((min(dx, n_x - dx), at))
    for dy in range(n_rows):
        for dh in range(2):
            for dl in range(2):
                if dy or dh or dl:
                    at = (4 * lax.rem(high_y + dy, n_rows) + 2 * lax.rem(high + dh, 2) + core, x, lax.rem(y + dl, 2))
                    hops = min(dy, n_rows - dy) + (1 if dl else 2 * dh)
                    far.append((hops, at))
    stages = [[at for _, at in sorted(stage, key=lambda item: -item[0])] for stage in (near, far)]

    barrier = pltpu.get_barrier_semaphore()
    friends = [(up, x, y), (down, x, y), (up, x, y_other), (down, x, y_other)]
    friends += [peer for stage in stages for peer in stage]
    for peer in friends:
        pl.semaphore_signal(barrier, inc=1, device_id=peer, device_id_type=MESH)

    def remote(a, b, s, t, device):
        return pltpu.make_async_remote_copy(a, b, s, t, device_id=device, device_id_type=MESH)

    arrays = ((labels, lab), (penalty, pen), (cap_source, src), (cap_sink, snk))
    loads = []

    def load(q):
        whole, held = arrays[q]
        for t in range(tiles):
            column = slice(t * LANES, (t + 1) * LANES)
            copy = pltpu.make_async_copy(whole.at[:, :, column], held.at[:, t, TOP:end, :], load_sem.at[q, t])
            copy.start()
            loads.append(copy)

    own_copy = pltpu.make_async_copy(multiplier.at[0], own_lam.at[TOP:end], lam_load_sem)
    own_copy.start()
    load(0)
    load(1)
    pl.semaphore_wait(barrier, len(friends))

    lam_bounds = [0] + [CHUNK * c - HALO for c in range(1, CHUNKS)] + [width_x]
    lam_copies = [
        remote(multiplier.at[0, a:b], low_lam.at[TOP + a : TOP + b], lam_send.at[c], lam_recv.at[c], (up, x, y))
        for c, (a, b) in enumerate(zip(lam_bounds[:-1], lam_bounds[1:]))
    ]
    lam_copies[0].start()

    sides = (
        ((r, x_prev, y), slice(0, TAKE), slice(0, TAKE), slice(end, end + HALO), slice(end, end + TAKE)),
        ((r, x_next, y), slice(width_x - TAKE, width_x), slice(HALO - TAKE, HALO), slice(TOP - HALO, TOP), slice(TOP - TAKE, TOP)),
    )
    halos = []

    def send_halo(q):
        for side, (device, take, put, _, _) in enumerate(sides):
            copy = remote(arrays[q][0].at[:, take, :], halo.at[q, side, :, put, :], halo_send.at[q, side], halo_recv.at[q, side], device)
            copy.start()
            halos.append(copy)

    def place_halo(q):
        for copy in halos[2 * q : 2 * q + 2]:
            copy.wait()
        for side, (_, _, _, put, _) in enumerate(sides):
            for z in range(depth):
                for t in range(tiles):
                    arrays[q][1][z, t, put, :] = halo[q, side, z, :, t * LANES : (t + 1) * LANES]

    def take_in(q):
        for copy in loads[q * tiles : (q + 1) * tiles]:
            copy.wait()
        place_halo(q)

    lam_halo = []
    for side, (device, take, _, _, put) in enumerate(sides):
        copy = remote(multiplier.at[0, take], own_lam.at[put], halo_send.at[4, side], halo_recv.at[4, side], device)
        copy.start()
        lam_halo.append(copy)
    send_halo(0)
    send_halo(1)
    load(2)
    load(3)
    send_halo(2)
    send_halo(3)

    has_above = (r < n_region - 1).astype(jnp.float32)
    has_below = (r > 0).astype(jnp.float32)
    not_first_x = (x > 0).astype(jnp.float32)
    is_last_x = x == n_x - 1
    lam_lane = SPAN * (depth - 1)
    edge_tile = (1 - y) * (tiles - 1)
    edge_column = pl.ds(pl.multiple_of(edge_tile * LANES, LANES), LANES)
    small = lane_of(8)

    def turned(value, shift):
        return pltpu.roll(value, lax.rem(shift + 4 * LANES, LANES), 1)

    own_copy.wait()
    for copy in lam_halo:
        copy.wait()
    forwards = []
    for n, (_, _, _, _, put) in enumerate(sides):
        copy = remote(own_lam.at[put], low_lam.at[put], fwd_send.at[n], fwd_recv.at[n], (up, x, y))
        copy.start()
        forwards.append(copy)

    for d in range(wide_rows // (8 * GROUPS)):
        value = None
        for g in range(GROUPS):
            row = first_row + 8 * (d * GROUPS + g)
            moved = turned(own_lam[row : row + 8, edge_column], 8 * g + 6 - 6 * y)
            value = moved if value is None else jnp.where(small >= 8 * g, moved, value)
        packed[8 * d : 8 * d + 8, :] = value
    for n, device in enumerate(((up, x, y), (up, x, y_other))):
        copy = remote(packed, packed_low.at[n], fwd_send.at[2 + n], fwd_recv.at[2 + n], device)
        copy.start()
        forwards.append(copy)

    for copy in lam_copies[1:]:
        copy.start()

    def hold_last(ref, *at):
        here = ref[(*at, pl.ds(end, 8), slice(None))]
        last = ref[(*at, pl.ds(end - 1, 8), slice(None))]
        ref[(*at, pl.ds(end, 8), slice(None))] = jnp.where(is_last_x, last, here)

    scale = STEP / CC

    def ascend(k, z, row, count):
        rows, after = pl.ds(row, count), pl.ds(row + 1, count)
        lane = lane_of(count)
        field = lab if k == 0 else jj
        here = [field[z, t, rows, :] for t in range(tiles)]
        rolled = [pltpu.roll(v, LANES - 1, 1) for v in here]
        for t in range(tiles):
            j = here[t]
            jx = field[z, t, after, :]
            jy = jnp.where(lane == LANES - 1, rolled[t + 1] if t < tiles - 1 else j, rolled[t])
            dx, dy = (jx - j, jy - j) if k else ((j - jx) * scale, (j - jy) * scale)
            qx, qy = (px[z, t, rows, :] + dx, py[z, t, rows, :] + dy) if k else (dx, dy)
            square = qx * qx + qy * qy
            jz = field[jnp.minimum(z + 1, depth - 1), t, rows, :]
            qz = pz[z, t, rows, :] + (jz - j) if k else (j - jz) * scale
            square = square + qz * qz
            factor = jnp.minimum(pen[z, t, rows, :] * lax.rsqrt(square), 1.0)
            px[z, t, rows, :] = qx * factor
            py[z, t, rows, :] = qy * factor
            pz[z, t, rows, :] = qz * factor

    def open_x(z):
        for t in range(tiles):
            px[z, t, first_row:TOP, :] = px[z, t, first_row:TOP, :] * not_first_x

    def close_x(z):
        for t in range(tiles):
            hold_last(jj, z, t)

    def descend(k, z, row, count, total=None, check=False):
        rows, before = pl.ds(row, count), pl.ds(row - 1, count)
        lane = lane_of(count)
        here = [py[z, t, rows, :] for t in range(tiles)]
        rolled = [pltpu.roll(v, 1, 1) for v in here]
        bottom = isinstance(z, int) and z == 0
        top = isinstance(z, int) and z == depth - 1
        if check:
            index = row + lax.broadcasted_iota(jnp.int32, (count, LANES), 0)
            inside = (index >= TOP) & (index < end)
        for t in range(tiles):
            columns = slice(t * LANES, (t + 1) * LANES)
            dv = px[z, t, rows, :] - px[z, t, before, :] + (here[t] - jnp.where(lane == 0, rolled[t - 1] if t else 0.0, rolled[t]))
            if not top:
                dv = dv + pz[z, t, rows, :]
            if not bottom:
                dv = dv - pz[z - 1, t, rows, :]
            source, sink = src[z, t, rows, :], snk[z, t, rows, :]
            if k:
                w, flow = lab[z, t, rows, :], pt[z, t, rows, :]
            else:
                if bottom:
                    sink = sink - low_lam[rows, columns] * has_below
                if top:
                    sink = sink + own_lam[rows, columns] * has_above
                if bottom or top:
                    snk[z, t, rows, :] = sink
                w, flow = lab[z, t, rows, :] * (1.0 / CC), jnp.minimum(source, sink)
            level = jnp.minimum(source - dv + w, flow + 1.0 / CC)
            after = jnp.maximum(level - sink, 0.0)
            if k < ITERS - 1:
                pt[z, t, rows, :] = jnp.minimum(sink, level)
                lab[z, t, rows, :] = after
                jj[z, t, rows, :] = w * STEP - after * (2.0 * STEP)
            else:
                out[z, rows, columns] = after * CC
                change = jnp.abs(w - after)
                if t == 0:
                    change = jnp.where((lane < 3) & (y == 1), 0.0, change)
                if t == tiles - 1:
                    change = jnp.where((lane >= LANES - 3) & (y == 0), 0.0, change)
                total = total + (jnp.where(inside, change, 0.0) if check else change)
        return total

    def planes(low, high, body, finish):
        def plane(z, carry):
            def step(i, inner):
                body(z, pl.multiple_of(first_row + i * WIDE, 8))
                return inner

            lax.fori_loop(0, steps, step, 0)
            finish(z)
            return carry

        if high - low == 1:
            plane(low, 0)
        else:
            lax.fori_loop(low, high, plane, 0)

    def ascend_planes(k, low, high):
        planes(low, high, lambda z, row: ascend(k, z, row, WIDE), open_x)

    def descend_planes(k, low, high):
        planes(low, high, lambda z, row: descend(k, z, row, WIDE), close_x)

    def side_step(body):
        body(first_row)

    side_lane = lane_of(wide_rows)

    def ascend_side(k):
        field = wj.at[k - 1] if k else wl

        def body(row):
            rows, after = pl.ds(row, wide_rows), pl.ds(row + 1, wide_rows)
            j = field[rows, :]
            jx = field[after, :]
            jy = pltpu.roll(j, LANES - 1, 1)
            jz = pltpu.roll(j, LANES - SPAN, 1)
            if k:
                qx = wpx[rows, :] + (jx - j)
                qy = wpy[k - 1, rows, :] + (jy - j)
                qz = wpz[rows, :] + (jz - j)
            else:
                qx, qy, qz = (j - jx) * scale, (j - jy) * scale, (j - jz) * scale
            qz = jnp.where(side_lane < lam_lane, qz, 0.0)
            factor = jnp.minimum(wp[rows, :] * lax.rsqrt(qx * qx + qy * qy + qz * qz), 1.0)
            wpx[rows, :] = qx * factor
            wpy[k, rows, :] = qy * factor
            wpz[rows, :] = qz * factor

        side_step(body)
        wpx[first_row:TOP, :] = wpx[first_row:TOP, :] * not_first_x

    def descend_side(k, total=None):
        def body(row):
            rows, before = pl.ds(row, wide_rows), pl.ds(row - 1, wide_rows)
            qy, qz = wpy[k, rows, :], wpz[rows, :]
            dv = wpx[rows, :] - wpx[before, :] + (qy - pltpu.roll(qy, 1, 1)) + (qz - pltpu.roll(qz, SPAN, 1))
            source, sink = ws[rows, :], wk[rows, :]
            if k:
                w, flow = ww[rows, :], wt[rows, :]
            else:
                w, flow = wl[rows, :] * (1.0 / CC), jnp.minimum(source, sink)
            level = jnp.minimum(source - dv + w, flow + 1.0 / CC)
            after = jnp.maximum(level - sink, 0.0)
            if k < ITERS - 1:
                wt[rows, :] = jnp.minimum(sink, level)
                ww[rows, :] = after
                wj[k, rows, :] = w * STEP - after * (2.0 * STEP)
            else:
                wu[rows, :] = after * CC
                j = side_lane & (SPAN - 1)
                index = row + lax.broadcasted_iota(jnp.int32, (wide_rows, LANES), 0)
                inside = (j >= 3) & (j < 6) & (index >= TOP) & (index < end)
                ww[rows, :] = jnp.where(inside, jnp.abs(w - after), 0.0)

        side_step(body)
        if k < ITERS - 1:
            hold_last(wj, k)

    take_in(0)
    take_in(1)
    for z in range(depth):
        for t in range(tiles):
            hold_last(lab, z, t)
    ascend_planes(0, 0, depth)
    take_in(2)
    take_in(3)
    side_lane_part = lane_of(WIDE)

    def own_window(i, carry):
        row = pl.multiple_of(first_row + i * WIDE, 8)
        rows = pl.ds(row, WIDE)
        for (_, held), strip in zip(arrays, (wl, wp, ws, wk)):
            value = None
            for z in range(depth):
                moved = turned(held[z, edge_tile, rows, :], SPAN * z + 6 - 3 * y)
                value = moved if value is None else jnp.where(side_lane_part >= SPAN * z, moved, value)
            if strip is wk:
                moved = turned(own_lam[rows, edge_column], lam_lane + 6 - 3 * y)
                value = value + jnp.where(side_lane_part >= lam_lane, moved * has_above, 0.0)
            strip[rows, :] = value
        return carry

    lax.fori_loop(0, steps, own_window, 0)
    def pack_window(i, carry):
        off = lane_of(WIDE // 2) & (SPAN - 1)
        value = None
        for g in range(steps):
            rows = pl.ds(pl.multiple_of(first_row + WIDE * g + i * (WIDE // 2), 8), WIDE // 2)
            moves = ((wl, 0, -3), (wp, 3, 0), (ws, 6, 2 + y), (wk, 8, 4 + y))
            for strip, at, shift in moves:
                moved = turned(strip[rows, :], PART * g + shift)
                value = moved if value is None else jnp.where(off >= PART * g + at, moved, value)
        sent[pl.ds(pl.multiple_of(i * (WIDE // 2), 8), WIDE // 2), :] = value
        return carry

    lax.fori_loop(0, 2, pack_window, 0)
    window = remote(sent, other, win_send, win_recv, (r, x, y_other))
    window.start()
    descend_planes(0, 1, depth - 1)
    ascend_planes(1, 1, 2)

    above_bounds = [0] + [CHUNK * c - 3 * HALO for c in range(1, CHUNKS)] + [width_x]
    above_copies = [
        remote(out.at[0, TOP + a : TOP + b], above.at[a:b], up_send.at[c], up_recv.at[c], (down, x, y))
        for c, (a, b) in enumerate(zip(above_bounds[:-1], above_bounds[1:]))
    ]

    for copy in forwards[:2]:
        copy.wait()

    def chunk(c, total):
        for n in range(CHUNKS):

            @pl.when(c == n)
            def _():
                lam_copies[n].wait()

        row = pl.multiple_of(first_row + c * CHUNK, 8)
        descend(0, 0, row, CHUNK)
        close_x(0)
        ascend(1, 0, row - 8, CHUNK)
        open_x(0)
        descend(1, 0, row - 8, CHUNK)
        descend(1, 1, row - 8, CHUNK)
        close_x(0)
        close_x(1)
        ascend(2, 0, row - 16, CHUNK)
        open_x(0)
        total = descend(2, 0, row - 16, CHUNK, total, True)
        for n in range(CHUNKS):

            @pl.when(c == n)
            def _():
                above_copies[n].start()

        return total

    total = lax.fori_loop(0, CHUNKS, chunk, jnp.zeros((CHUNK, LANES), jnp.float32))
    err_row = jnp.sum(total, axis=0, keepdims=True)

    window.wait()
    for copy in forwards[2:]:
        copy.wait()
    for g in range(steps):
        rows = slice(first_row + WIDE * g, first_row + WIDE * (g + 1))
        off = side_lane_part & (SPAN - 1)
        theirs = (off >= 6 - 6 * y) & (off < 9 - 6 * y)
        moves = ((wl, 6 - 6 * y), (wp, 3 - 6 * y), (ws, -5 * y), (wk, -2 - 5 * y))
        for strip, shift in moves:
            strip[rows, :] = jnp.where(theirs, turned(other[...], shift - PART * g), strip[rows, :])
    hold_last(wl)
    for n in range(wide_rows // 8):
        d, g = n // GROUPS, n % GROUPS
        rows = slice(first_row + 8 * n, first_row + 8 * n + 8)
        same = turned(packed_low[0, 8 * d : 8 * d + 8, :], 3 * y - 8 * g)
        cross = turned(packed_low[1, 8 * d : 8 * d + 8, :], 6 - 9 * y - 8 * g)
        theirs = (small >= 6 - 6 * y) & (small < 9 - 6 * y)
        lam = jnp.where(theirs, cross, same)
        wk[rows, :] = wk[rows, :] - jnp.where(small < 9, lam * has_below, 0.0)
    for k in range(ITERS):
        ascend_side(k)
        descend_side(k)
    for d in range(wide_rows // (8 * GROUPS)):
        value = None
        for g in range(GROUPS):
            row = first_row + 8 * (d * GROUPS + g)
            moved = pltpu.roll(wu[row : row + 8, :], 8 * g, 1)
            value = moved if value is None else jnp.where(small >= 8 * g, moved, value)
        packed_u[8 * d : 8 * d + 8, :] = value
    down_copy = remote(packed_u, packed_above, fwd_send.at[4], fwd_recv.at[4], (down, x, y))
    down_copy.start()
    err_row = err_row + jnp.sum(ww[first_row : end + HALO, :], axis=0, keepdims=True)

    descend_planes(0, depth - 1, depth)
    ascend_planes(1, 2, depth)
    descend_planes(1, 2, depth)
    ascend_planes(2, 1, depth)

    def last_plane(z, carry):
        def step(i, inner):
            return descend(ITERS - 1, z, pl.multiple_of(TOP + i * BLOCK, 8), BLOCK, inner)

        return lax.fori_loop(0, width_x // BLOCK, step, carry)

    total = lax.fori_loop(1, depth, last_plane, jnp.zeros((BLOCK, LANES), jnp.float32))
    err_row = err_row + jnp.sum(total, axis=0, keepdims=True)

    def edge_of(rows):
        lane = lane_of(rows)
        return (lane >= (1 - y) * (LANES - 3)) & (lane < (1 - y) * (LANES - 3) + 3)

    def patch(z):
        moved = turned(wu[TOP:end, :], 122 - 125 * y - SPAN * z)
        out[z, TOP:end, edge_column] = jnp.where(edge_of(width_x), moved, out[z, TOP:end, edge_column])

    for z in range(1, depth):
        patch(z)
    down_copy.wait()

    gaps = jnp.zeros((8, LANES), jnp.float32)
    edge = edge_of(8)
    for copy, a, b in zip(above_copies, above_bounds[:-1], above_bounds[1:]):
        copy.wait()
        for row in range(a, b, 8):
            n = row // 8 + 1
            d, g = n // GROUPS, n % GROUPS
            moved = turned(packed_above[8 * d : 8 * d + 8, :], 122 - 125 * y - 8 * g)
            above[row : row + 8, edge_column] = jnp.where(edge, moved, above[row : row + 8, edge_column])
        gap = (out[depth - 1, TOP + a : TOP + b, :] - above[a:b, :]) * has_above
        above[a:b, :] = gap
        squares = gap * gap
        for row in range(0, b - a, 8):
            for t in range(tiles):
                gaps = gaps + squares[row : row + 8, t * LANES : (t + 1) * LANES]
    gap_row = jnp.sum(gaps, axis=0, keepdims=True)
    sub = lax.broadcasted_iota(jnp.int32, (8, LANES), 0)
    mine = jnp.where(sub == 0, gap_row, jnp.where(sub == 1, err_row, 0.0))
    sends = []
    for s, (stage, got) in enumerate(zip(stages, (got_near, got_far))):
        part[s] = mine
        for n, peer in enumerate(stage):
            copy = remote(part.at[s, 0:2], got.at[n, 0:2], red_send.at[s, n], red_recv.at[s], peer)
            copy.start()
            sends.append(copy)
        if s == len(stages) - 1:
            patch(0)
        pltpu.make_async_copy(got.at[:, 0:2], got.at[:, 0:2], red_recv.at[s]).wait()
        mine = mine + jnp.sum(got[...], axis=0)
    for copy in sends:
        copy.wait_send()

    sums = jnp.sum(mine, axis=1, keepdims=True)
    all_cells = depth * width_x * width_y * n_region * n_x * n_y
    plane_cells = (n_region - 1) * width_x * n_x * width_y * n_y
    err = sums[1:2, :] * (CC / all_cells)
    msq = sums[0:1, :] * (1.0 / plane_cells)
    rate = RHO * err * lax.rsqrt(msq + EPSILON)

    def write(i, carry):
        rows = pl.ds(pl.multiple_of(i * BLOCK, 8), BLOCK)
        lam_rows = pl.ds(pl.multiple_of(TOP + i * BLOCK, 8), BLOCK)
        mult[0, rows, :] = own_lam[lam_rows, :] * has_above + above[rows, :] * rate
        return carry

    lax.fori_loop(0, width_x // BLOCK, write, 0)


def write_out(held, held_mult, out, mult, sem):
    depth, width_x, _ = out.shape
    copies = [pltpu.make_async_copy(held.at[z, TOP : TOP + width_x], out.at[z], sem.at[z]) for z in range(depth)]
    copies.append(pltpu.make_async_copy(held_mult, mult, sem.at[depth]))
    for copy in copies:
        copy.start()
    for copy in copies:
        copy.wait()


def on_device(sizes, cap_source, cap_sink, penalty, labels, multiplier):
    depth, width_x, width_y = labels.shape
    tiles = width_y // LANES
    rows = TOP + width_x + BOTTOM
    n_region, n_x, n_y = sizes

    def vmem(*shape):
        return pltpu.VMEM(shape, jnp.float32)

    def dma(*shape):
        return pltpu.SemaphoreType.DMA(shape) if shape else pltpu.SemaphoreType.DMA

    volume = vmem(depth, tiles, rows, LANES)
    plane = vmem(rows, width_y)
    strip = vmem(rows, LANES)
    third = vmem((width_x + 2 * HALO) // 3, LANES)
    near, far = 2 * n_x - 1, n_region - 1
    compact = (width_x + 2 * HALO) // GROUPS
    held, held_mult = pl.pallas_call(
        functools.partial(kernel, sizes),
        out_shape=[
            pltpu.VMEM((depth, rows, width_y), jnp.float32),
            pltpu.VMEM(multiplier.shape, jnp.float32),
        ],
        in_specs=[pl.BlockSpec(memory_space=pl.ANY)] * 5,
        out_specs=[pl.BlockSpec(memory_space=pltpu.VMEM)] * 2,
        scratch_shapes=[
            volume,
            volume,
            volume,
            volume,
            volume,
            volume,
            volume,
            volume,
            volume,
            plane,
            plane,
            vmem(width_x, width_y),
            vmem(4, 2, depth, HALO, width_y),
            third,
            third,
            strip,
            strip,
            strip,
            strip,
            strip,
            strip,
            strip,
            strip,
            vmem(2, rows, LANES),
            vmem(3, rows, LANES),
            strip,
            vmem(compact, LANES),
            vmem(2, compact, LANES),
            vmem(compact, LANES),
            vmem(compact, LANES),
            vmem(2, 8, LANES),
            vmem(near, 8, LANES),
            vmem(far, 8, LANES),
            dma(4, tiles),
            dma(),
            dma(5, 2),
            dma(5, 2),
            dma(CHUNKS),
            dma(CHUNKS),
            dma(),
            dma(),
            dma(5),
            dma(5),
            dma(CHUNKS),
            dma(CHUNKS),
            dma(2, far),
            dma(2),
        ],
        compiler_params=pltpu.CompilerParams(collective_id=0, has_side_effects=True, vmem_limit_bytes=52 << 20),
        name="slab_flow",
    )(cap_source, cap_sink, penalty, labels, multiplier)
    return pl.pallas_call(
        write_out,
        out_shape=[
            jax.ShapeDtypeStruct(labels.shape, jnp.float32),
            jax.ShapeDtypeStruct(multiplier.shape, jnp.float32),
        ],
        in_specs=[pl.BlockSpec(memory_space=pl.ANY)] * 2,
        out_specs=[pl.BlockSpec(memory_space=pl.ANY)] * 2,
        scratch_shapes=[dma(depth + 1)],
        compiler_params=pltpu.CompilerParams(vmem_limit_bytes=4 << 20),
        name="write_out",
    )(held, held_mult)


def solution(mesh):
    placed = P("region", "gx", "gy")
    sizes = tuple(mesh.shape[a] for a in ("region", "gx", "gy"))
    return jax.shard_map(
        functools.partial(on_device, sizes),
        mesh=mesh,
        in_specs=(placed,) * 5,
        out_specs=(placed, placed),
        check_vma=False,
    )
```

```python
import functools

import jax
import jax.numpy as jnp
from jax import lax
from jax.experimental import pallas as pl
from jax.experimental.pallas import tpu as pltpu
from jax.sharding import PartitionSpec as P

MESH = pl.DeviceIdType.MESH
ITERS = 3
CC = 0.3
STEP = 0.16
RHO = 0.5
EPSILON = 1e-06

LANES = 128
TOP = 32
BOTTOM = 32
HALO = 8
TAKE = 4
SPAN = 32
PART = 10
GROUPS = 11
WIDE = 176
BLOCK = 256
CHUNKS = 3
CHUNK = 184
EARLY = 9


def lane_of(rows):
    return lax.broadcasted_iota(jnp.int32, (rows, LANES), 1)


def kernel(
    sizes,
    cap_source,
    cap_sink,
    penalty,
    labels,
    multiplier,
    out,
    mult,
    lab,
    src,
    snk,
    pen,
    px,
    py,
    pz,
    jj,
    pt,
    own_lam,
    low_lam,
    above,
    halo,
    sent,
    other,
    wl,
    wp,
    ws,
    wk,
    ww,
    wt,
    wpx,
    wpz,
    wj,
    wpy,
    wu,
    packed,
    packed_low,
    packed_u,
    packed_above,
    part,
    got_near,
    got_far,
    load_sem,
    lam_load_sem,
    halo_send,
    halo_recv,
    lam_send,
    lam_recv,
    win_send,
    win_recv,
    fwd_send,
    fwd_recv,
    up_send,
    up_recv,
    red_send,
    red_recv,
):
    n_region, n_x, n_y = sizes
    depth, width_x, width_y = labels.shape
    tiles = width_y // LANES
    end = TOP + width_x
    first_row = TOP - HALO
    wide_rows = width_x + 2 * HALO
    steps = wide_rows // WIDE
    r, x, y = lax.axis_index("region"), lax.axis_index("gx"), lax.axis_index("gy")
    up, down = lax.rem(r + 1, n_region), lax.rem(r + n_region - 1, n_region)
    x_next, x_prev = lax.rem(x + 1, n_x), lax.rem(x + n_x - 1, n_x)
    y_other = 1 - y
    core, high, high_y = lax.rem(r, 2), lax.rem(r // 2, 2), r // 4
    n_rows = n_region // 4
    near, far = [], []
    for dx in range(n_x):
        for dc in range(2):
            if dx or dc:
                at = (4 * high_y + 2 * high + lax.rem(core + dc, 2), lax.rem(x + dx, n_x), y)
                near.append((min(dx, n_x - dx), at))
    for dy in range(n_rows):
        for dh in range(2):
            for dl in range(2):
                if dy or dh or dl:
                    at = (4 * lax.rem(high_y + dy, n_rows) + 2 * lax.rem(high + dh, 2) + core, x, lax.rem(y + dl, 2))
                    hops = min(dy, n_rows - dy) + (1 if dl else 2 * dh)
                    far.append((hops, at))
    stages = [[at for _, at in sorted(stage, key=lambda item: -item[0])] for stage in (near, far)]

    barrier = pltpu.get_barrier_semaphore()
    friends = [(up, x, y), (down, x, y), (up, x, y_other), (down, x, y_other)]
    friends += [peer for stage in stages for peer in stage]
    friends.sort(key=lambda peer: peer[1] is x)

    def greet(peers):
        for peer in peers:
            pl.semaphore_signal(barrier, inc=1, device_id=peer, device_id_type=MESH)

    def remote(a, b, s, t, device):
        return pltpu.make_async_remote_copy(a, b, s, t, device_id=device, device_id_type=MESH)

    arrays = ((labels, lab), (penalty, pen), (cap_source, src), (cap_sink, snk))
    loads = []

    def load(q):
        whole, held = arrays[q]
        for t in range(tiles):
            column = slice(t * LANES, (t + 1) * LANES)
            copy = pltpu.make_async_copy(whole.at[:, :, column], held.at[:, t, TOP:end, :], load_sem.at[q, t])
            copy.start()
            loads.append(copy)

    own_copy = pltpu.make_async_copy(multiplier.at[0], own_lam.at[TOP:end], lam_load_sem)
    greet(friends[:EARLY])
    own_copy.start()
    load(0)
    load(1)
    greet(friends[EARLY:])
    pl.semaphore_wait(barrier, len(friends))

    lam_bounds = [0] + [CHUNK * c - HALO for c in range(1, CHUNKS)] + [width_x]
    lam_copies = [
        remote(multiplier.at[0, a:b], low_lam.at[TOP + a : TOP + b], lam_send.at[c], lam_recv.at[c], (up, x, y))
        for c, (a, b) in enumerate(zip(lam_bounds[:-1], lam_bounds[1:]))
    ]
    lam_copies[0].start()

    sides = (
        ((r, x_prev, y), slice(0, TAKE), slice(0, TAKE), slice(end, end + HALO), slice(end, end + TAKE)),
        ((r, x_next, y), slice(width_x - TAKE, width_x), slice(HALO - TAKE, HALO), slice(TOP - HALO, TOP), slice(TOP - TAKE, TOP)),
    )
    halos = []

    def send_halo(q):
        for side, (device, take, put, _, _) in enumerate(sides):
            copy = remote(arrays[q][0].at[:, take, :], halo.at[q, side, :, put, :], halo_send.at[q, side], halo_recv.at[q, side], device)
            copy.start()
            halos.append(copy)

    def place_halo(q):
        for copy in halos[2 * q : 2 * q + 2]:
            copy.wait()
        for side, (_, _, _, put, _) in enumerate(sides):
            for z in range(depth):
                for t in range(tiles):
                    arrays[q][1][z, t, put, :] = halo[q, side, z, :, t * LANES : (t + 1) * LANES]

    def take_in(q):
        for copy in loads[q * tiles : (q + 1) * tiles]:
            copy.wait()
        place_halo(q)

    lam_halo = []
    for side, (device, take, _, _, put) in enumerate(sides):
        copy = remote(multiplier.at[0, take], own_lam.at[put], halo_send.at[4, side], halo_recv.at[4, side], device)
        copy.start()
        lam_halo.append(copy)
    send_halo(0)
    send_halo(1)
    load(2)
    load(3)
    send_halo(2)
    send_halo(3)

    has_above = (r < n_region - 1).astype(jnp.float32)
    has_below = (r > 0).astype(jnp.float32)
    not_first_x = (x > 0).astype(jnp.float32)
    is_last_x = x == n_x - 1
    lam_lane = SPAN * (depth - 1)
    edge_tile = (1 - y) * (tiles - 1)
    edge_column = pl.ds(pl.multiple_of(edge_tile * LANES, LANES), LANES)
    small = lane_of(8)

    def turned(value, shift):
        return pltpu.roll(value, lax.rem(shift + 4 * LANES, LANES), 1)

    own_copy.wait()
    for copy in lam_halo:
        copy.wait()
    forwards = []
    for n, (_, _, _, _, put) in enumerate(sides):
        copy = remote(own_lam.at[put], low_lam.at[put], fwd_send.at[n], fwd_recv.at[n], (up, x, y))
        copy.start()
        forwards.append(copy)

    for d in range(wide_rows // (8 * GROUPS)):
        value = None
        for g in range(GROUPS):
            row = first_row + 8 * (d * GROUPS + g)
            moved = turned(own_lam[row : row + 8, edge_column], 8 * g + 6 - 6 * y)
            value = moved if value is None else jnp.where(small >= 8 * g, moved, value)
        packed[8 * d : 8 * d + 8, :] = value
    for n, device in enumerate(((up, x, y), (up, x, y_other))):
        copy = remote(packed, packed_low.at[n], fwd_send.at[2 + n], fwd_recv.at[2 + n], device)
        copy.start()
        forwards.append(copy)

    for copy in lam_copies[1:]:
        copy.start()

    def hold_last(ref, *at):
        here = ref[(*at, pl.ds(end, 8), slice(None))]
        last = ref[(*at, pl.ds(end - 1, 8), slice(None))]
        ref[(*at, pl.ds(end, 8), slice(None))] = jnp.where(is_last_x, last, here)

    scale = STEP / CC

    def ascend(k, z, row, count):
        rows, after = pl.ds(row, count), pl.ds(row + 1, count)
        lane = lane_of(count)
        field = lab if k == 0 else jj
        here = [field[z, t, rows, :] for t in range(tiles)]
        rolled = [pltpu.roll(v, LANES - 1, 1) for v in here]
        for t in range(tiles):
            j = here[t]
            jx = field[z, t, after, :]
            jy = jnp.where(lane == LANES - 1, rolled[t + 1] if t < tiles - 1 else j, rolled[t])
            dx, dy = (jx - j, jy - j) if k else ((j - jx) * scale, (j - jy) * scale)
            qx, qy = (px[z, t, rows, :] + dx, py[z, t, rows, :] + dy) if k else (dx, dy)
            square = qx * qx + qy * qy
            jz = field[jnp.minimum(z + 1, depth - 1), t, rows, :]
            qz = pz[z, t, rows, :] + (jz - j) if k else (j - jz) * scale
            square = square + qz * qz
            factor = jnp.minimum(pen[z, t, rows, :] * lax.rsqrt(square), 1.0)
            px[z, t, rows, :] = qx * factor
            py[z, t, rows, :] = qy * factor
            pz[z, t, rows, :] = qz * factor

    def open_x(z):
        for t in range(tiles):
            px[z, t, first_row:TOP, :] = px[z, t, first_row:TOP, :] * not_first_x

    def close_x(z):
        for t in range(tiles):
            hold_last(jj, z, t)

    def descend(k, z, row, count, total=None, check=False):
        rows, before = pl.ds(row, count), pl.ds(row - 1, count)
        lane = lane_of(count)
        here = [py[z, t, rows, :] for t in range(tiles)]
        rolled = [pltpu.roll(v, 1, 1) for v in here]
        bottom = isinstance(z, int) and z == 0
        top = isinstance(z, int) and z == depth - 1
        if check:
            index = row + lax.broadcasted_iota(jnp.int32, (count, LANES), 0)
            inside = (index >= TOP) & (index < end)
        for t in range(tiles):
            columns = slice(t * LANES, (t + 1) * LANES)
            dv = px[z, t, rows, :] - px[z, t, before, :] + (here[t] - jnp.where(lane == 0, rolled[t - 1] if t else 0.0, rolled[t]))
            if not top:
                dv = dv + pz[z, t, rows, :]
            if not bottom:
                dv = dv - pz[z - 1, t, rows, :]
            source, sink = src[z, t, rows, :], snk[z, t, rows, :]
            if k:
                w, flow = lab[z, t, rows, :], pt[z, t, rows, :]
            else:
                if bottom:
                    sink = sink - low_lam[rows, columns] * has_below
                if top:
                    sink = sink + own_lam[rows, columns] * has_above
                if bottom or top:
                    snk[z, t, rows, :] = sink
                w, flow = lab[z, t, rows, :] * (1.0 / CC), jnp.minimum(source, sink)
            level = jnp.minimum(source - dv + w, flow + 1.0 / CC)
            after = jnp.maximum(level - sink, 0.0)
            if k < ITERS - 1:
                pt[z, t, rows, :] = jnp.minimum(sink, level)
                lab[z, t, rows, :] = after
                jj[z, t, rows, :] = w * STEP - after * (2.0 * STEP)
            else:
                out[z, rows, columns] = after * CC
                change = jnp.abs(w - after)
                if t == 0:
                    change = jnp.where((lane < 3) & (y == 1), 0.0, change)
                if t == tiles - 1:
                    change = jnp.where((lane >= LANES - 3) & (y == 0), 0.0, change)
                total = total + (jnp.where(inside, change, 0.0) if check else change)
        return total

    def planes(low, high, body, finish):
        def plane(z, carry):
            def step(i, inner):
                body(z, pl.multiple_of(first_row + i * WIDE, 8))
                return inner

            lax.fori_loop(0, steps, step, 0)
            finish(z)
            return carry

        if high - low == 1:
            plane(low, 0)
        else:
            lax.fori_loop(low, high, plane, 0)

    def ascend_planes(k, low, high):
        planes(low, high, lambda z, row: ascend(k, z, row, WIDE), open_x)

    def descend_planes(k, low, high):
        planes(low, high, lambda z, row: descend(k, z, row, WIDE), close_x)

    def side_step(body):
        body(first_row)

    side_lane = lane_of(wide_rows)

    def ascend_side(k):
        field = wj.at[k - 1] if k else wl

        def body(row):
            rows, after = pl.ds(row, wide_rows), pl.ds(row + 1, wide_rows)
            j = field[rows, :]
            jx = field[after, :]
            jy = pltpu.roll(j, LANES - 1, 1)
            jz = pltpu.roll(j, LANES - SPAN, 1)
            if k:
                qx = wpx[rows, :] + (jx - j)
                qy = wpy[k - 1, rows, :] + (jy - j)
                qz = wpz[rows, :] + (jz - j)
            else:
                qx, qy, qz = (j - jx) * scale, (j - jy) * scale, (j - jz) * scale
            qz = jnp.where(side_lane < lam_lane, qz, 0.0)
            factor = jnp.minimum(wp[rows, :] * lax.rsqrt(qx * qx + qy * qy + qz * qz), 1.0)
            wpx[rows, :] = qx * factor
            wpy[k, rows, :] = qy * factor
            wpz[rows, :] = qz * factor

        side_step(body)
        wpx[first_row:TOP, :] = wpx[first_row:TOP, :] * not_first_x

    def descend_side(k, total=None):
        def body(row):
            rows, before = pl.ds(row, wide_rows), pl.ds(row - 1, wide_rows)
            qy, qz = wpy[k, rows, :], wpz[rows, :]
            dv = wpx[rows, :] - wpx[before, :] + (qy - pltpu.roll(qy, 1, 1)) + (qz - pltpu.roll(qz, SPAN, 1))
            source, sink = ws[rows, :], wk[rows, :]
            if k:
                w, flow = ww[rows, :], wt[rows, :]
            else:
                w, flow = wl[rows, :] * (1.0 / CC), jnp.minimum(source, sink)
            level = jnp.minimum(source - dv + w, flow + 1.0 / CC)
            after = jnp.maximum(level - sink, 0.0)
            if k < ITERS - 1:
                wt[rows, :] = jnp.minimum(sink, level)
                ww[rows, :] = after
                wj[k, rows, :] = w * STEP - after * (2.0 * STEP)
            else:
                wu[rows, :] = after * CC
                j = side_lane & (SPAN - 1)
                index = row + lax.broadcasted_iota(jnp.int32, (wide_rows, LANES), 0)
                inside = (j >= 3) & (j < 6) & (index >= TOP) & (index < end)
                ww[rows, :] = jnp.where(inside, jnp.abs(w - after), 0.0)

        side_step(body)
        if k < ITERS - 1:
            hold_last(wj, k)

    take_in(0)
    take_in(1)
    for z in range(depth):
        for t in range(tiles):
            hold_last(lab, z, t)
    ascend_planes(0, 0, depth)
    take_in(2)
    take_in(3)
    side_lane_part = lane_of(WIDE)

    def own_window(row):
        rows = pl.ds(row, wide_rows)
        for (_, held), strip in zip(arrays, (wl, wp, ws, wk)):
            value = None
            for z in range(depth):
                moved = turned(held[z, edge_tile, rows, :], SPAN * z + 6 - 3 * y)
                value = moved if value is None else jnp.where(side_lane >= SPAN * z, moved, value)
            if strip is wk:
                moved = turned(own_lam[rows, edge_column], lam_lane + 6 - 3 * y)
                value = value + jnp.where(side_lane >= lam_lane, moved * has_above, 0.0)
            strip[rows, :] = value

    side_step(own_window)
    def pack_window(i, carry):
        off = lane_of(WIDE // 2) & (SPAN - 1)
        value = None
        for g in range(steps):
            rows = pl.ds(pl.multiple_of(first_row + WIDE * g + i * (WIDE // 2), 8), WIDE // 2)
            moves = ((wl, 0, -3), (wp, 3, 0), (ws, 6, 2 + y), (wk, 8, 4 + y))
            for strip, at, shift in moves:
                moved = turned(strip[rows, :], PART * g + shift)
                value = moved if value is None else jnp.where(off >= PART * g + at, moved, value)
        sent[pl.ds(pl.multiple_of(i * (WIDE // 2), 8), WIDE // 2), :] = value
        return carry

    lax.fori_loop(0, 2, pack_window, 0)
    window = remote(sent, other, win_send, win_recv, (r, x, y_other))
    window.start()
    descend_planes(0, 1, depth - 1)
    ascend_planes(1, 1, 2)

    above_bounds = [0] + [CHUNK * c - 3 * HALO for c in range(1, CHUNKS)] + [width_x]
    above_copies = [
        remote(out.at[0, TOP + a : TOP + b], above.at[a:b], up_send.at[c], up_recv.at[c], (down, x, y))
        for c, (a, b) in enumerate(zip(above_bounds[:-1], above_bounds[1:]))
    ]

    for copy in forwards[:2]:
        copy.wait()

    def chunk(c, total):
        @pl.when(c == CHUNKS - 1)
        def _():
            descend_planes(0, depth - 1, depth)
            ascend_planes(1, 2, depth)

        for n in range(CHUNKS):

            @pl.when(c == n)
            def _():
                lam_copies[n].wait()

        row = pl.multiple_of(first_row + c * CHUNK, 8)
        descend(0, 0, row, CHUNK)
        close_x(0)
        ascend(1, 0, row - 8, CHUNK)
        open_x(0)
        descend(1, 0, row - 8, CHUNK)
        descend(1, 1, row - 8, CHUNK)
        close_x(0)
        close_x(1)
        ascend(2, 0, row - 16, CHUNK)
        open_x(0)
        total = descend(2, 0, row - 16, CHUNK, total, True)
        for n in range(CHUNKS):

            @pl.when(c == n)
            def _():
                above_copies[n].start()

        return total

    total = lax.fori_loop(0, CHUNKS, chunk, jnp.zeros((CHUNK, LANES), jnp.float32))
    err_row = jnp.sum(total, axis=0, keepdims=True)

    window.wait()
    for copy in forwards[2:]:
        copy.wait()
    for g in range(steps):
        rows = slice(first_row + WIDE * g, first_row + WIDE * (g + 1))
        off = side_lane_part & (SPAN - 1)
        theirs = (off >= 6 - 6 * y) & (off < 9 - 6 * y)
        moves = ((wl, 6 - 6 * y), (wp, 3 - 6 * y), (ws, -5 * y), (wk, -2 - 5 * y))
        for strip, shift in moves:
            strip[rows, :] = jnp.where(theirs, turned(other[...], shift - PART * g), strip[rows, :])
    hold_last(wl)
    for n in range(wide_rows // 8):
        d, g = n // GROUPS, n % GROUPS
        rows = slice(first_row + 8 * n, first_row + 8 * n + 8)
        same = turned(packed_low[0, 8 * d : 8 * d + 8, :], 3 * y - 8 * g)
        cross = turned(packed_low[1, 8 * d : 8 * d + 8, :], 6 - 9 * y - 8 * g)
        theirs = (small >= 6 - 6 * y) & (small < 9 - 6 * y)
        lam = jnp.where(theirs, cross, same)
        wk[rows, :] = wk[rows, :] - jnp.where(small < 9, lam * has_below, 0.0)
    for k in range(ITERS):
        ascend_side(k)
        descend_side(k)
    for d in range(wide_rows // (8 * GROUPS)):
        value = None
        for g in range(GROUPS):
            row = first_row + 8 * (d * GROUPS + g)
            moved = pltpu.roll(wu[row : row + 8, :], 8 * g, 1)
            value = moved if value is None else jnp.where(small >= 8 * g, moved, value)
        packed_u[8 * d : 8 * d + 8, :] = value
    down_copy = remote(packed_u, packed_above, fwd_send.at[4], fwd_recv.at[4], (down, x, y))
    down_copy.start()
    err_row = err_row + jnp.sum(ww[first_row : end + HALO, :], axis=0, keepdims=True)

    descend_planes(1, 2, depth)
    ascend_planes(2, 1, depth)

    def last_plane(z, carry):
        def step(i, inner):
            return descend(ITERS - 1, z, pl.multiple_of(TOP + i * BLOCK, 8), BLOCK, inner)

        return lax.fori_loop(0, width_x // BLOCK, step, carry)

    total = lax.fori_loop(1, depth, last_plane, jnp.zeros((BLOCK, LANES), jnp.float32))
    err_row = err_row + jnp.sum(total, axis=0, keepdims=True)

    def edge_of(rows):
        lane = lane_of(rows)
        return (lane >= (1 - y) * (LANES - 3)) & (lane < (1 - y) * (LANES - 3) + 3)

    def patch(z):
        moved = turned(wu[TOP:end, :], 122 - 125 * y - SPAN * z)
        out[z, TOP:end, edge_column] = jnp.where(edge_of(width_x), moved, out[z, TOP:end, edge_column])

    for z in range(1, depth):
        patch(z)
    down_copy.wait()

    gaps = [jnp.zeros((8, LANES), jnp.float32)] * (2 * tiles)
    edge = edge_of(8)
    for copy, a, b in zip(above_copies, above_bounds[:-1], above_bounds[1:]):
        copy.wait()
        for row in range(a, b, 8):
            n = row // 8 + 1
            d, g = n // GROUPS, n % GROUPS
            moved = turned(packed_above[8 * d : 8 * d + 8, :], 122 - 125 * y - 8 * g)
            above[row : row + 8, edge_column] = jnp.where(edge, moved, above[row : row + 8, edge_column])
        gap = (out[depth - 1, TOP + a : TOP + b, :] - above[a:b, :]) * has_above
        above[a:b, :] = gap
        squares = gap * gap
        for row in range(0, b - a, 8):
            for t in range(tiles):
                n = 2 * t + row // 8 % 2
                gaps[n] = gaps[n] + squares[row : row + 8, t * LANES : (t + 1) * LANES]
    gap_row = jnp.sum(sum(gaps[1:], gaps[0]), axis=0, keepdims=True)
    sub = lax.broadcasted_iota(jnp.int32, (8, LANES), 0)
    mine = jnp.where(sub == 0, gap_row, jnp.where(sub == 1, err_row, 0.0))
    sends = []
    for s, (stage, got) in enumerate(zip(stages, (got_near, got_far))):
        part[s] = mine
        for n, peer in enumerate(stage):
            copy = remote(part.at[s, 0:2], got.at[n, 0:2], red_send.at[s, n], red_recv.at[s], peer)
            copy.start()
            sends.append(copy)
        if s == len(stages) - 1:
            patch(0)
        pltpu.make_async_copy(got.at[:, 0:2], got.at[:, 0:2], red_recv.at[s]).wait()
        mine = mine + jnp.sum(got[...], axis=0)
    for copy in sends:
        copy.wait_send()

    sums = jnp.sum(mine, axis=1, keepdims=True)
    all_cells = depth * width_x * width_y * n_region * n_x * n_y
    plane_cells = (n_region - 1) * width_x * n_x * width_y * n_y
    err = sums[1:2, :] * (CC / all_cells)
    msq = sums[0:1, :] * (1.0 / plane_cells)
    rate = RHO * err * lax.rsqrt(msq + EPSILON)

    mult[0] = own_lam[TOP:end, :] * has_above + above[...] * rate


def write_out(held, held_mult, out, mult, sem):
    depth, width_x, _ = out.shape
    copies = [pltpu.make_async_copy(held.at[z, TOP : TOP + width_x], out.at[z], sem.at[z]) for z in range(depth)]
    copies.append(pltpu.make_async_copy(held_mult, mult, sem.at[depth]))
    for copy in copies:
        copy.start()
    for copy in copies:
        copy.wait()


def on_device(sizes, cap_source, cap_sink, penalty, labels, multiplier):
    depth, width_x, width_y = labels.shape
    tiles = width_y // LANES
    rows = TOP + width_x + BOTTOM
    n_region, n_x, n_y = sizes

    def vmem(*shape):
        return pltpu.VMEM(shape, jnp.float32)

    def dma(*shape):
        return pltpu.SemaphoreType.DMA(shape) if shape else pltpu.SemaphoreType.DMA

    volume = vmem(depth, tiles, rows, LANES)
    plane = vmem(rows, width_y)
    strip = vmem(rows, LANES)
    third = vmem((width_x + 2 * HALO) // 3, LANES)
    near, far = 2 * n_x - 1, n_region - 1
    compact = (width_x + 2 * HALO) // GROUPS
    held, held_mult = pl.pallas_call(
        functools.partial(kernel, sizes),
        out_shape=[
            pltpu.VMEM((depth, rows, width_y), jnp.float32),
            pltpu.VMEM(multiplier.shape, jnp.float32),
        ],
        in_specs=[pl.BlockSpec(memory_space=pl.ANY)] * 5,
        out_specs=[pl.BlockSpec(memory_space=pltpu.VMEM)] * 2,
        scratch_shapes=[
            volume,
            volume,
            volume,
            volume,
            volume,
            volume,
            volume,
            volume,
            volume,
            plane,
            plane,
            vmem(width_x, width_y),
            vmem(4, 2, depth, HALO, width_y),
            third,
            third,
            strip,
            strip,
            strip,
            strip,
            strip,
            strip,
            strip,
            strip,
            vmem(2, rows, LANES),
            vmem(3, rows, LANES),
            strip,
            vmem(compact, LANES),
            vmem(2, compact, LANES),
            vmem(compact, LANES),
            vmem(compact, LANES),
            vmem(2, 8, LANES),
            vmem(near, 8, LANES),
            vmem(far, 8, LANES),
            dma(4, tiles),
            dma(),
            dma(5, 2),
            dma(5, 2),
            dma(CHUNKS),
            dma(CHUNKS),
            dma(),
            dma(),
            dma(5),
            dma(5),
            dma(CHUNKS),
            dma(CHUNKS),
            dma(2, far),
            dma(2),
        ],
        compiler_params=pltpu.CompilerParams(collective_id=0, has_side_effects=True, vmem_limit_bytes=52 << 20),
        name="slab_flow",
    )(cap_source, cap_sink, penalty, labels, multiplier)
    return pl.pallas_call(
        write_out,
        out_shape=[
            jax.ShapeDtypeStruct(labels.shape, jnp.float32),
            jax.ShapeDtypeStruct(multiplier.shape, jnp.float32),
        ],
        in_specs=[pl.BlockSpec(memory_space=pl.ANY)] * 2,
        out_specs=[pl.BlockSpec(memory_space=pl.ANY)] * 2,
        scratch_shapes=[dma(depth + 1)],
        compiler_params=pltpu.CompilerParams(vmem_limit_bytes=4 << 20),
        name="write_out",
    )(held, held_mult)


def solution(mesh):
    placed = P("region", "gx", "gy")
    sizes = tuple(mesh.shape[a] for a in ("region", "gx", "gy"))
    return jax.shard_map(
        functools.partial(on_device, sizes),
        mesh=mesh,
        in_specs=(placed,) * 5,
        out_specs=(placed, placed),
        check_vma=False,
    )
```

```python
import functools

import jax
import jax.numpy as jnp
from jax import lax
from jax.experimental import pallas as pl
from jax.experimental.pallas import tpu as pltpu
from jax.sharding import PartitionSpec as P

MESH = pl.DeviceIdType.MESH
ITERS = 3
CC = 0.3
STEP = 0.16
RHO = 0.5
EPSILON = 1e-06

LANES = 128
TOP = 32
BOTTOM = 32
HALO = 8
TAKE = 4
SPAN = 32
PART = 10
GROUPS = 11
WIDE = 176
BLOCK = 128
CHUNKS = 3
CHUNK = 184
EARLY = 9


def lane_of(rows):
    return lax.broadcasted_iota(jnp.int32, (rows, LANES), 1)


def kernel(
    sizes,
    cap_source,
    cap_sink,
    penalty,
    labels,
    multiplier,
    out,
    mult,
    lab,
    src,
    snk,
    pen,
    px,
    py,
    pz,
    jj,
    pt,
    own_lam,
    low_lam,
    above,
    halo,
    sent,
    other,
    wl,
    wp,
    ws,
    wk,
    ww,
    wt,
    wpx,
    wpz,
    wj,
    wpy,
    wu,
    packed,
    packed_low,
    packed_u,
    packed_above,
    part,
    got_near,
    got_far,
    load_sem,
    lam_load_sem,
    halo_send,
    halo_recv,
    lam_send,
    lam_recv,
    win_send,
    win_recv,
    fwd_send,
    fwd_recv,
    up_send,
    up_recv,
    red_send,
    red_recv,
):
    n_region, n_x, n_y = sizes
    depth, width_x, width_y = labels.shape
    tiles = width_y // LANES
    end = TOP + width_x
    first_row = TOP - HALO
    wide_rows = width_x + 2 * HALO
    steps = wide_rows // WIDE
    r, x, y = lax.axis_index("region"), lax.axis_index("gx"), lax.axis_index("gy")
    up, down = lax.rem(r + 1, n_region), lax.rem(r + n_region - 1, n_region)
    x_next, x_prev = lax.rem(x + 1, n_x), lax.rem(x + n_x - 1, n_x)
    y_other = 1 - y
    core, high, high_y = lax.rem(r, 2), lax.rem(r // 2, 2), r // 4
    n_rows = n_region // 4
    near, far = [], []
    for dx in range(n_x):
        for dc in range(2):
            if dx or dc:
                at = (4 * high_y + 2 * high + lax.rem(core + dc, 2), lax.rem(x + dx, n_x), y)
                near.append((min(dx, n_x - dx), at))
    for dy in range(n_rows):
        for dh in range(2):
            for dl in range(2):
                if dy or dh or dl:
                    at = (4 * lax.rem(high_y + dy, n_rows) + 2 * lax.rem(high + dh, 2) + core, x, lax.rem(y + dl, 2))
                    hops = min(dy, n_rows - dy) + (1 if dl else 2 * dh)
                    far.append((hops, at))
    stages = [[at for _, at in sorted(stage, key=lambda item: -item[0])] for stage in (near, far)]

    barrier = pltpu.get_barrier_semaphore()
    friends = [(up, x, y), (down, x, y), (up, x, y_other), (down, x, y_other)]
    friends += [peer for stage in stages for peer in stage]
    friends.sort(key=lambda peer: peer[1] is x)

    def greet(peers):
        for peer in peers:
            pl.semaphore_signal(barrier, inc=1, device_id=peer, device_id_type=MESH)

    def remote(a, b, s, t, device):
        return pltpu.make_async_remote_copy(a, b, s, t, device_id=device, device_id_type=MESH)

    arrays = ((labels, lab), (penalty, pen), (cap_source, src), (cap_sink, snk))
    loads = []

    def load(q):
        whole, held = arrays[q]
        for t in range(tiles):
            column = slice(t * LANES, (t + 1) * LANES)
            copy = pltpu.make_async_copy(whole.at[:, :, column], held.at[:, t, TOP:end, :], load_sem.at[q, t])
            copy.start()
            loads.append(copy)

    own_copy = pltpu.make_async_copy(multiplier.at[0], own_lam.at[TOP:end], lam_load_sem)
    greet(friends[:EARLY])
    own_copy.start()
    load(0)
    load(1)
    greet(friends[EARLY:])
    pl.semaphore_wait(barrier, len(friends))

    lam_bounds = [0] + [CHUNK * c - HALO for c in range(1, CHUNKS)] + [width_x]
    lam_copies = [
        remote(multiplier.at[0, a:b], low_lam.at[TOP + a : TOP + b], lam_send.at[c], lam_recv.at[c], (up, x, y))
        for c, (a, b) in enumerate(zip(lam_bounds[:-1], lam_bounds[1:]))
    ]
    lam_copies[0].start()

    sides = (
        ((r, x_prev, y), slice(0, TAKE), slice(0, TAKE), slice(end, end + HALO), slice(end, end + TAKE)),
        ((r, x_next, y), slice(width_x - TAKE, width_x), slice(HALO - TAKE, HALO), slice(TOP - HALO, TOP), slice(TOP - TAKE, TOP)),
    )
    halos = []

    def send_halo(q):
        for side, (device, take, put, _, _) in enumerate(sides):
            copy = remote(arrays[q][0].at[:, take, :], halo.at[q, side, :, put, :], halo_send.at[q, side], halo_recv.at[q, side], device)
            copy.start()
            halos.append(copy)

    def place_halo(q):
        for copy in halos[2 * q : 2 * q + 2]:
            copy.wait()
        for side, (_, _, _, put, _) in enumerate(sides):
            for z in range(depth):
                for t in range(tiles):
                    arrays[q][1][z, t, put, :] = halo[q, side, z, :, t * LANES : (t + 1) * LANES]

    def take_in(q):
        for copy in loads[q * tiles : (q + 1) * tiles]:
            copy.wait()
        place_halo(q)

    lam_halo = []
    for side, (device, take, _, _, put) in enumerate(sides):
        copy = remote(multiplier.at[0, take], own_lam.at[put], halo_send.at[4, side], halo_recv.at[4, side], device)
        copy.start()
        lam_halo.append(copy)
    send_halo(0)
    send_halo(1)
    load(2)
    load(3)
    send_halo(2)
    send_halo(3)

    has_above = (r < n_region - 1).astype(jnp.float32)
    has_below = (r > 0).astype(jnp.float32)
    not_first_x = (x > 0).astype(jnp.float32)
    is_last_x = x == n_x - 1
    lam_lane = SPAN * (depth - 1)
    edge_tile = (1 - y) * (tiles - 1)
    edge_column = pl.ds(pl.multiple_of(edge_tile * LANES, LANES), LANES)
    small = lane_of(8)

    def turned(value, shift):
        return pltpu.roll(value, lax.rem(shift + 4 * LANES, LANES), 1)

    own_copy.wait()
    for copy in lam_halo:
        copy.wait()
    forwards = []
    for n, (_, _, _, _, put) in enumerate(sides):
        copy = remote(own_lam.at[put], low_lam.at[put], fwd_send.at[n], fwd_recv.at[n], (up, x, y))
        copy.start()
        forwards.append(copy)

    for d in range(wide_rows // (8 * GROUPS)):
        value = None
        for g in range(GROUPS):
            row = first_row + 8 * (d * GROUPS + g)
            moved = turned(own_lam[row : row + 8, edge_column], 8 * g + 6 - 6 * y)
            value = moved if value is None else jnp.where(small >= 8 * g, moved, value)
        packed[8 * d : 8 * d + 8, :] = value
    for n, device in enumerate(((up, x, y), (up, x, y_other))):
        copy = remote(packed, packed_low.at[n], fwd_send.at[2 + n], fwd_recv.at[2 + n], device)
        copy.start()
        forwards.append(copy)

    for copy in lam_copies[1:]:
        copy.start()

    def hold_last(ref, *at):
        here = ref[(*at, pl.ds(end, 8), slice(None))]
        last = ref[(*at, pl.ds(end - 1, 8), slice(None))]
        ref[(*at, pl.ds(end, 8), slice(None))] = jnp.where(is_last_x, last, here)

    scale = STEP / CC

    def ascend(k, z, row, count):
        rows, after = pl.ds(row, count), pl.ds(row + 1, count)
        lane = lane_of(count)
        field = lab if k == 0 else jj
        here = [field[z, t, rows, :] for t in range(tiles)]
        rolled = [pltpu.roll(v, LANES - 1, 1) for v in here]
        for t in range(tiles):
            j = here[t]
            jx = field[z, t, after, :]
            jy = jnp.where(lane == LANES - 1, rolled[t + 1] if t < tiles - 1 else j, rolled[t])
            dx, dy = (jx - j, jy - j) if k else ((j - jx) * scale, (j - jy) * scale)
            qx, qy = (px[z, t, rows, :] + dx, py[z, t, rows, :] + dy) if k else (dx, dy)
            square = qx * qx + qy * qy
            jz = field[jnp.minimum(z + 1, depth - 1), t, rows, :]
            qz = pz[z, t, rows, :] + (jz - j) if k else (j - jz) * scale
            square = square + qz * qz
            factor = jnp.minimum(pen[z, t, rows, :] * lax.rsqrt(square), 1.0)
            px[z, t, rows, :] = qx * factor
            py[z, t, rows, :] = qy * factor
            pz[z, t, rows, :] = qz * factor

    def open_x(z):
        for t in range(tiles):
            px[z, t, first_row:TOP, :] = px[z, t, first_row:TOP, :] * not_first_x

    def close_x(z):
        for t in range(tiles):
            hold_last(jj, z, t)

    def descend(k, z, row, count, total=None, check=False):
        rows, before = pl.ds(row, count), pl.ds(row - 1, count)
        lane = lane_of(count)
        here = [py[z, t, rows, :] for t in range(tiles)]
        rolled = [pltpu.roll(v, 1, 1) for v in here]
        bottom = isinstance(z, int) and z == 0
        top = isinstance(z, int) and z == depth - 1
        if check:
            index = row + lax.broadcasted_iota(jnp.int32, (count, LANES), 0)
            inside = (index >= TOP) & (index < end)
        for t in range(tiles):
            columns = slice(t * LANES, (t + 1) * LANES)
            dv = px[z, t, rows, :] - px[z, t, before, :] + (here[t] - jnp.where(lane == 0, rolled[t - 1] if t else 0.0, rolled[t]))
            if not top:
                dv = dv + pz[z, t, rows, :]
            if not bottom:
                dv = dv - pz[z - 1, t, rows, :]
            source, sink = src[z, t, rows, :], snk[z, t, rows, :]
            if k:
                w, flow = lab[z, t, rows, :], pt[z, t, rows, :]
            else:
                if bottom:
                    sink = sink - low_lam[rows, columns] * has_below
                if top:
                    sink = sink + own_lam[rows, columns] * has_above
                if bottom or top:
                    snk[z, t, rows, :] = sink
                w, flow = lab[z, t, rows, :] * (1.0 / CC), jnp.minimum(source, sink)
            level = jnp.minimum(source - dv + w, flow + 1.0 / CC)
            after = jnp.maximum(level - sink, 0.0)
            if k < ITERS - 1:
                pt[z, t, rows, :] = jnp.minimum(sink, level)
                lab[z, t, rows, :] = after
                jj[z, t, rows, :] = w * STEP - after * (2.0 * STEP)
            else:
                out[z, rows, columns] = after * CC
                change = jnp.abs(w - after)
                if t == 0:
                    change = jnp.where((lane < 3) & (y == 1), 0.0, change)
                if t == tiles - 1:
                    change = jnp.where((lane >= LANES - 3) & (y == 0), 0.0, change)
                total = total + (jnp.where(inside, change, 0.0) if check else change)
        return total

    def planes(low, high, body, finish):
        def plane(z, carry):
            def step(i, inner):
                body(z, pl.multiple_of(first_row + i * WIDE, 8))
                return inner

            lax.fori_loop(0, steps, step, 0)
            finish(z)
            return carry

        if high - low == 1:
            plane(low, 0)
        else:
            lax.fori_loop(low, high, plane, 0)

    def ascend_planes(k, low, high):
        planes(low, high, lambda z, row: ascend(k, z, row, WIDE), open_x)

    def descend_planes(k, low, high):
        planes(low, high, lambda z, row: descend(k, z, row, WIDE), close_x)

    def side_step(body):
        body(first_row)

    side_lane = lane_of(wide_rows)

    def ascend_side(k):
        field = wj.at[k - 1] if k else wl

        def body(row):
            rows, after = pl.ds(row, wide_rows), pl.ds(row + 1, wide_rows)
            j = field[rows, :]
            jx = field[after, :]
            jy = pltpu.roll(j, LANES - 1, 1)
            jz = pltpu.roll(j, LANES - SPAN, 1)
            if k:
                qx = wpx[rows, :] + (jx - j)
                qy = wpy[k - 1, rows, :] + (jy - j)
                qz = wpz[rows, :] + (jz - j)
            else:
                qx, qy, qz = (j - jx) * scale, (j - jy) * scale, (j - jz) * scale
            qz = jnp.where(side_lane < lam_lane, qz, 0.0)
            factor = jnp.minimum(wp[rows, :] * lax.rsqrt(qx * qx + qy * qy + qz * qz), 1.0)
            wpx[rows, :] = qx * factor
            wpy[k, rows, :] = qy * factor
            wpz[rows, :] = qz * factor

        side_step(body)
        wpx[first_row:TOP, :] = wpx[first_row:TOP, :] * not_first_x

    def descend_side(k, total=None):
        def body(row):
            rows, before = pl.ds(row, wide_rows), pl.ds(row - 1, wide_rows)
            qy, qz = wpy[k, rows, :], wpz[rows, :]
            dv = wpx[rows, :] - wpx[before, :] + (qy - pltpu.roll(qy, 1, 1)) + (qz - pltpu.roll(qz, SPAN, 1))
            source, sink = ws[rows, :], wk[rows, :]
            if k:
                w, flow = ww[rows, :], wt[rows, :]
            else:
                w, flow = wl[rows, :] * (1.0 / CC), jnp.minimum(source, sink)
            level = jnp.minimum(source - dv + w, flow + 1.0 / CC)
            after = jnp.maximum(level - sink, 0.0)
            if k < ITERS - 1:
                wt[rows, :] = jnp.minimum(sink, level)
                ww[rows, :] = after
                wj[k, rows, :] = w * STEP - after * (2.0 * STEP)
            else:
                wu[rows, :] = after * CC
                j = side_lane & (SPAN - 1)
                index = row + lax.broadcasted_iota(jnp.int32, (wide_rows, LANES), 0)
                inside = (j >= 3) & (j < 6) & (index >= TOP) & (index < end)
                ww[rows, :] = jnp.where(inside, jnp.abs(w - after), 0.0)

        side_step(body)
        if k < ITERS - 1:
            hold_last(wj, k)

    take_in(0)
    take_in(1)
    for z in range(depth):
        for t in range(tiles):
            hold_last(lab, z, t)
    ascend_planes(0, 0, depth)
    take_in(2)
    take_in(3)
    side_lane_part = lane_of(WIDE)

    def own_window(row):
        rows = pl.ds(row, wide_rows)
        for (_, held), strip in zip(arrays, (wl, wp, ws, wk)):
            value = None
            for z in range(depth):
                moved = turned(held[z, edge_tile, rows, :], SPAN * z + 6 - 3 * y)
                value = moved if value is None else jnp.where(side_lane >= SPAN * z, moved, value)
            if strip is wk:
                moved = turned(own_lam[rows, edge_column], lam_lane + 6 - 3 * y)
                value = value + jnp.where(side_lane >= lam_lane, moved * has_above, 0.0)
            strip[rows, :] = value

    side_step(own_window)
    def pack_window(i, carry):
        off = lane_of(WIDE // 2) & (SPAN - 1)
        value = None
        for g in range(steps):
            rows = pl.ds(pl.multiple_of(first_row + WIDE * g + i * (WIDE // 2), 8), WIDE // 2)
            moves = ((wl, 0, -3), (wp, 3, 0), (ws, 6, 2 + y), (wk, 8, 4 + y))
            for strip, at, shift in moves:
                moved = turned(strip[rows, :], PART * g + shift)
                value = moved if value is None else jnp.where(off >= PART * g + at, moved, value)
        sent[pl.ds(pl.multiple_of(i * (WIDE // 2), 8), WIDE // 2), :] = value
        return carry

    lax.fori_loop(0, 2, pack_window, 0)
    window = remote(sent, other, win_send, win_recv, (r, x, y_other))
    window.start()
    descend_planes(0, 1, depth - 1)
    ascend_planes(1, 1, 2)

    above_bounds = [0] + [CHUNK * c - 3 * HALO for c in range(1, CHUNKS)] + [width_x]
    above_copies = [
        remote(out.at[0, TOP + a : TOP + b], above.at[a:b], up_send.at[c], up_recv.at[c], (down, x, y))
        for c, (a, b) in enumerate(zip(above_bounds[:-1], above_bounds[1:]))
    ]

    for copy in forwards[:2]:
        copy.wait()

    def chunk(c, total):
        @pl.when(c == CHUNKS - 1)
        def _():
            descend_planes(0, depth - 1, depth)
            ascend_planes(1, 2, depth)

        for n in range(CHUNKS):

            @pl.when(c == n)
            def _():
                lam_copies[n].wait()

        row = pl.multiple_of(first_row + c * CHUNK, 8)
        descend(0, 0, row, CHUNK)
        close_x(0)
        ascend(1, 0, row - 8, CHUNK)
        open_x(0)
        descend(1, 0, row - 8, CHUNK)
        descend(1, 1, row - 8, CHUNK)
        close_x(0)
        close_x(1)
        ascend(2, 0, row - 16, CHUNK)
        open_x(0)
        total = descend(2, 0, row - 16, CHUNK, total, True)
        for n in range(CHUNKS):

            @pl.when(c == n)
            def _():
                above_copies[n].start()

        return total

    total = lax.fori_loop(0, CHUNKS, chunk, jnp.zeros((CHUNK, LANES), jnp.float32))
    err_row = jnp.sum(total, axis=0, keepdims=True)

    window.wait()
    for copy in forwards[2:]:
        copy.wait()
    for g in range(steps):
        rows = slice(first_row + WIDE * g, first_row + WIDE * (g + 1))
        off = side_lane_part & (SPAN - 1)
        theirs = (off >= 6 - 6 * y) & (off < 9 - 6 * y)
        moves = ((wl, 6 - 6 * y), (wp, 3 - 6 * y), (ws, -5 * y), (wk, -2 - 5 * y))
        for strip, shift in moves:
            strip[rows, :] = jnp.where(theirs, turned(other[...], shift - PART * g), strip[rows, :])
    hold_last(wl)
    for n in range(wide_rows // 8):
        d, g = n // GROUPS, n % GROUPS
        rows = slice(first_row + 8 * n, first_row + 8 * n + 8)
        same = turned(packed_low[0, 8 * d : 8 * d + 8, :], 3 * y - 8 * g)
        cross = turned(packed_low[1, 8 * d : 8 * d + 8, :], 6 - 9 * y - 8 * g)
        theirs = (small >= 6 - 6 * y) & (small < 9 - 6 * y)
        lam = jnp.where(theirs, cross, same)
        wk[rows, :] = wk[rows, :] - jnp.where(small < 9, lam * has_below, 0.0)
    for k in range(ITERS):
        ascend_side(k)
        descend_side(k)
    for d in range(wide_rows // (8 * GROUPS)):
        value = None
        for g in range(GROUPS):
            row = first_row + 8 * (d * GROUPS + g)
            moved = pltpu.roll(wu[row : row + 8, :], 8 * g, 1)
            value = moved if value is None else jnp.where(small >= 8 * g, moved, value)
        packed_u[8 * d : 8 * d + 8, :] = value
    down_copy = remote(packed_u, packed_above, fwd_send.at[4], fwd_recv.at[4], (down, x, y))
    down_copy.start()
    err_row = err_row + jnp.sum(ww[first_row : end + HALO, :], axis=0, keepdims=True)

    descend_planes(1, 2, depth)

    def finish(z, row, count, total):
        rows, after, before = pl.ds(row, count), pl.ds(row + 1, count), pl.ds(row - 1, count)
        lane = lane_of(count)
        here = [jj[z, t, rows, :] for t in range(tiles)]
        rolled = [pltpu.roll(v, LANES - 1, 1) for v in here]
        flows = []
        for t in range(tiles):
            j = here[t]
            jy = jnp.where(lane == LANES - 1, rolled[t + 1] if t < tiles - 1 else j, rolled[t])
            qx = px[z, t, rows, :] + (jj[z, t, after, :] - j)
            qy = py[z, t, rows, :] + (jy - j)
            qz = pz[z, t, rows, :] + (jj[jnp.minimum(z + 1, depth - 1), t, rows, :] - j)
            factor = jnp.minimum(pen[z, t, rows, :] * lax.rsqrt(qx * qx + qy * qy + qz * qz), 1.0)
            qx, qy, qz = qx * factor, qy * factor, qz * factor
            px[z, t, rows, :] = qx
            pz[z, t, rows, :] = qz
            flows.append((qx, qy, qz))
        turned_y = [pltpu.roll(flow[1], 1, 1) for flow in flows]
        for t in range(tiles):
            qx, qy, qz = flows[t]
            dv = qx - px[z, t, before, :] + (qy - jnp.where(lane == 0, turned_y[t - 1] if t else 0.0, turned_y[t]))
            dv = dv + qz - pz[z - 1, t, rows, :]
            sink, w = snk[z, t, rows, :], lab[z, t, rows, :]
            level = jnp.minimum(src[z, t, rows, :] - dv + w, pt[z, t, rows, :] + 1.0 / CC)
            new = jnp.maximum(level - sink, 0.0)
            out[z, rows, t * LANES : (t + 1) * LANES] = new * CC
            change = jnp.abs(w - new)
            if t == 0:
                change = jnp.where((lane < 3) & (y == 1), 0.0, change)
            if t == tiles - 1:
                change = jnp.where((lane >= LANES - 3) & (y == 0), 0.0, change)
            total = total + change
        return total

    def last_plane(z, carry):
        ascend(2, z, first_row, HALO)
        open_x(z)

        def step(i, inner):
            return finish(z, pl.multiple_of(TOP + i * BLOCK, 8), BLOCK, inner)

        return lax.fori_loop(0, width_x // BLOCK, step, carry)

    total = lax.fori_loop(1, depth, last_plane, jnp.zeros((BLOCK, LANES), jnp.float32))
    err_row = err_row + jnp.sum(total, axis=0, keepdims=True)

    def edge_of(rows):
        lane = lane_of(rows)
        return (lane >= (1 - y) * (LANES - 3)) & (lane < (1 - y) * (LANES - 3) + 3)

    def patch(z):
        moved = turned(wu[TOP:end, :], 122 - 125 * y - SPAN * z)
        out[z, TOP:end, edge_column] = jnp.where(edge_of(width_x), moved, out[z, TOP:end, edge_column])

    for z in range(1, depth):
        patch(z)
    down_copy.wait()

    gaps = [jnp.zeros((8, LANES), jnp.float32)] * (2 * tiles)
    edge = edge_of(8)
    for copy, a, b in zip(above_copies, above_bounds[:-1], above_bounds[1:]):
        copy.wait()
        for row in range(a, b, 8):
            n = row // 8 + 1
            d, g = n // GROUPS, n % GROUPS
            moved = turned(packed_above[8 * d : 8 * d + 8, :], 122 - 125 * y - 8 * g)
            above[row : row + 8, edge_column] = jnp.where(edge, moved, above[row : row + 8, edge_column])
        gap = (out[depth - 1, TOP + a : TOP + b, :] - above[a:b, :]) * has_above
        above[a:b, :] = gap
        squares = gap * gap
        for row in range(0, b - a, 8):
            for t in range(tiles):
                n = 2 * t + row // 8 % 2
                gaps[n] = gaps[n] + squares[row : row + 8, t * LANES : (t + 1) * LANES]
    gap_row = jnp.sum(sum(gaps[1:], gaps[0]), axis=0, keepdims=True)
    sub = lax.broadcasted_iota(jnp.int32, (8, LANES), 0)
    mine = jnp.where(sub == 0, gap_row, jnp.where(sub == 1, err_row, 0.0))
    sends = []
    for s, (stage, got) in enumerate(zip(stages, (got_near, got_far))):
        part[s] = mine
        for n, peer in enumerate(stage):
            copy = remote(part.at[s, 0:2], got.at[n, 0:2], red_send.at[s, n], red_recv.at[s], peer)
            copy.start()
            sends.append(copy)
        if s == len(stages) - 1:
            patch(0)
        pltpu.make_async_copy(got.at[:, 0:2], got.at[:, 0:2], red_recv.at[s]).wait()
        mine = mine + jnp.sum(got[...], axis=0)
    for copy in sends:
        copy.wait_send()

    sums = jnp.sum(mine, axis=1, keepdims=True)
    all_cells = depth * width_x * width_y * n_region * n_x * n_y
    plane_cells = (n_region - 1) * width_x * n_x * width_y * n_y
    err = sums[1:2, :] * (CC / all_cells)
    msq = sums[0:1, :] * (1.0 / plane_cells)
    rate = RHO * err * lax.rsqrt(msq + EPSILON)

    mult[0] = own_lam[TOP:end, :] * has_above + above[...] * rate


def write_out(held, held_mult, out, mult, sem):
    depth, width_x, _ = out.shape
    copies = [pltpu.make_async_copy(held.at[z, TOP : TOP + width_x], out.at[z], sem.at[z]) for z in range(depth)]
    copies.append(pltpu.make_async_copy(held_mult, mult, sem.at[depth]))
    for copy in copies:
        copy.start()
    for copy in copies:
        copy.wait()


def on_device(sizes, cap_source, cap_sink, penalty, labels, multiplier):
    depth, width_x, width_y = labels.shape
    tiles = width_y // LANES
    rows = TOP + width_x + BOTTOM
    n_region, n_x, n_y = sizes

    def vmem(*shape):
        return pltpu.VMEM(shape, jnp.float32)

    def dma(*shape):
        return pltpu.SemaphoreType.DMA(shape) if shape else pltpu.SemaphoreType.DMA

    volume = vmem(depth, tiles, rows, LANES)
    plane = vmem(rows, width_y)
    strip = vmem(rows, LANES)
    third = vmem((width_x + 2 * HALO) // 3, LANES)
    near, far = 2 * n_x - 1, n_region - 1
    compact = (width_x + 2 * HALO) // GROUPS
    held, held_mult = pl.pallas_call(
        functools.partial(kernel, sizes),
        out_shape=[
            pltpu.VMEM((depth, rows, width_y), jnp.float32),
            pltpu.VMEM(multiplier.shape, jnp.float32),
        ],
        in_specs=[pl.BlockSpec(memory_space=pl.ANY)] * 5,
        out_specs=[pl.BlockSpec(memory_space=pltpu.VMEM)] * 2,
        scratch_shapes=[
            volume,
            volume,
            volume,
            volume,
            volume,
            volume,
            volume,
            volume,
            volume,
            plane,
            plane,
            vmem(width_x, width_y),
            vmem(4, 2, depth, HALO, width_y),
            third,
            third,
            strip,
            strip,
            strip,
            strip,
            strip,
            strip,
            strip,
            strip,
            vmem(2, rows, LANES),
            vmem(3, rows, LANES),
            strip,
            vmem(compact, LANES),
            vmem(2, compact, LANES),
            vmem(compact, LANES),
            vmem(compact, LANES),
            vmem(2, 8, LANES),
            vmem(near, 8, LANES),
            vmem(far, 8, LANES),
            dma(4, tiles),
            dma(),
            dma(5, 2),
            dma(5, 2),
            dma(CHUNKS),
            dma(CHUNKS),
            dma(),
            dma(),
            dma(5),
            dma(5),
            dma(CHUNKS),
            dma(CHUNKS),
            dma(2, far),
            dma(2),
        ],
        compiler_params=pltpu.CompilerParams(collective_id=0, has_side_effects=True, vmem_limit_bytes=52 << 20),
        name="slab_flow",
    )(cap_source, cap_sink, penalty, labels, multiplier)
    return pl.pallas_call(
        write_out,
        out_shape=[
            jax.ShapeDtypeStruct(labels.shape, jnp.float32),
            jax.ShapeDtypeStruct(multiplier.shape, jnp.float32),
        ],
        in_specs=[pl.BlockSpec(memory_space=pl.ANY)] * 2,
        out_specs=[pl.BlockSpec(memory_space=pl.ANY)] * 2,
        scratch_shapes=[dma(depth + 1)],
        compiler_params=pltpu.CompilerParams(vmem_limit_bytes=4 << 20),
        name="write_out",
    )(held, held_mult)


def solution(mesh):
    placed = P("region", "gx", "gy")
    sizes = tuple(mesh.shape[a] for a in ("region", "gx", "gy"))
    return jax.shard_map(
        functools.partial(on_device, sizes),
        mesh=mesh,
        in_specs=(placed,) * 5,
        out_specs=(placed, placed),
        check_vma=False,
    )
```
